256 devices in a mesh: section: 2 (over core), item: 128 (over y, x, z).
Axes of the slice: x: 4, y: 4, z: 8, core: 2. Of those that a mesh axis runs over, the one named last changes fastest.
Arguments:
- history: bfloat16 [128, 1024, 1024], P('item', 'section'), may hold values from -12 to 12
- hist_len: int32 [128], P('item'), may hold values from 16 to 1024
- cand_ids: int32 [128, 768], P('item', 'section'), may hold values from 0 to 524287, as said below
- cand_count: int32 [128], P('item'), may hold values from 192 to 768
- table: bfloat16 [524288, 512], P('item'), may hold values from -6 to 6
- w_event: bfloat16 [1024, 1024], replicated, may hold values from -0.1875 to 0.1875
- w_kv: bfloat16 [1024, 1024], replicated, may hold values from -0.1875 to 0.1875
- pool_query: bfloat16 [1024], replicated, may hold values from -8 to 8
- w_rank: bfloat16 [2048, 512], replicated, may hold values from -0.125 to 0.125
- w_out: float32 [512], replicated, may hold values from -0.25 to 0.25
Outputs:
- scores: float32 [128, 768], P('item', 'section')
- user_state: bfloat16 [128, 1024], P('item')
The draws below stay inside these ranges and needn't reach their ends.
Inputs may be any that keep to these rules, and one draw needn't show every extreme that they name: `cand_ids`: every id is a row of the table; its owner is id // 4096. Among the 384 slots that one device holds (its requests' half of the candidate slots), at most 6 ids have the same owner, and in every device's slots one owner has exactly 6.
All inputs are finite; a program needn't handle non-finite values.
Results may differ from the reference program's by a relative error of at most 0.025.
Values may be sent and summed in bfloat16 or wider, within the bound.
A program may use at most 64 MiB of HBM per device.

```python
import math
import jax
import jax.numpy as jnp
from jax import lax

D = 1024
E = 512
RH = 512
HEAD = 128
HIST = 1024
CAND = 768
REQ_DEV = 1
ROWS_DEV = 4096
REQS = 128
ROWS = 524288
PH = 8
TH = 4
N_SECTION = 2
N_ITEM = 128


def spread_lengths(key, count_max, count_min, total):
    key_draw, key_place = jax.random.split(key)
    lengths = jax.random.randint(key_draw, (total,), count_min, count_max + 1)
    place = jax.random.randint(key_place, (), 0, total)
    lengths = lengths.at[place].set(count_max)
    lengths = lengths.at[(place + 1) % total].set(count_min)
    return lengths.astype(jnp.int32)


def draw_history(key, part):
    key = jax.random.fold_in(key, 11)
    key_body = jax.random.fold_in(key, 1)
    values = jnp.clip(jax.random.normal(key_body, (REQS, HIST, D), jnp.float32), -6.0, 6.0)
    return values.astype(jnp.bfloat16)


def draw_pool_query(key, part):
    key = jax.random.fold_in(key, 12)
    values = jnp.clip(jax.random.normal(key, (D,), jnp.float32), -4.0, 4.0)
    return values.astype(jnp.bfloat16)


def draw_table(key, part):
    key = jax.random.fold_in(key, 13)
    key_body = jax.random.fold_in(key, 1)
    values = jnp.clip(jax.random.normal(key_body, (ROWS, E), jnp.float32), -6.0, 6.0)
    return values.astype(jnp.bfloat16)


def draw_hist_len(key, part):
    key = jax.random.fold_in(key, 14)
    return spread_lengths(key, HIST, max(1, HIST // 64), REQS)


def draw_cand_count(key, part):
    key = jax.random.fold_in(key, 15)
    return spread_lengths(key, CAND, CAND // 4, REQS)


def draw_cand_ids(key, part):
    key = jax.random.fold_in(key, 16)
    slot_count = REQ_DEV * (CAND // N_SECTION)
    bound = 2 * slot_count // N_ITEM

    def one_block(block_key, block_number):
        key_hot, key_perm, key_offset = jax.random.split(block_key, 3)
        hot_owner = jax.random.randint(key_hot, (), 0, N_ITEM)
        hot_owner = jnp.where(block_number == 0, N_ITEM - 1, jnp.where(block_number == 1, 0, hot_owner))
        positions = jnp.arange(slot_count)
        other_owner = (positions - bound) % (N_ITEM - 1)
        other_owner = other_owner + (other_owner >= hot_owner).astype(jnp.int32)
        owner_base = jnp.where(positions < bound, hot_owner, other_owner)
        order = jax.random.permutation(key_perm, slot_count)
        owner_ids = owner_base[order]
        offsets = jax.random.randint(key_offset, (slot_count,), 0, ROWS_DEV)
        offsets = jnp.where(order == 0, ROWS_DEV - 1, jnp.where(order == 1, 0, offsets))
        return (owner_ids * ROWS_DEV + offsets).astype(jnp.int32)
    block_total = N_ITEM * N_SECTION
    blocks = jax.vmap(one_block)(jax.random.split(key, block_total), jnp.arange(block_total))
    blocks = blocks.reshape(N_ITEM, N_SECTION, REQ_DEV, CAND // N_SECTION)
    return blocks.transpose(0, 2, 1, 3).reshape(REQS, CAND)


def noise(stream_key, dims, deviation, most, dtype=jnp.bfloat16):
    array = jax.random.normal(stream_key, dims, jnp.float32) * deviation
    return jnp.minimum(jnp.maximum(array, -most), most).astype(dtype)


def setup_inputs(seed: int = 0) -> dict:
    key_of = jax.random.split(jax.random.key(seed), 11)
    return {
        "history": draw_history(jax.random.fold_in(key_of[10], 71), 0),
        "hist_len": draw_hist_len(jax.random.fold_in(key_of[10], 71), 0),
        "cand_ids": draw_cand_ids(jax.random.fold_in(key_of[10], 71), 0),
        "cand_count": draw_cand_count(jax.random.fold_in(key_of[10], 71), 0),
        "table": draw_table(jax.random.fold_in(key_of[10], 71), 0),
        "w_event": noise(key_of[5], (D, D), D ** -0.5, 0.1875),
        "w_kv": noise(key_of[6], (D, 2 * E), D ** -0.5, 0.1875),
        "pool_query": draw_pool_query(jax.random.fold_in(key_of[10], 71), 0),
        "w_rank": noise(key_of[8], (2 * E + D, RH), (2 * E + D) ** -0.5, 0.125),
        "w_out": noise(key_of[9], (RH,), RH ** -0.5, 0.25, jnp.float32),
    }


masked_value = -1e+30

def softmax_rows(score_grid, valid_mask):
    score_grid = jnp.where(valid_mask, score_grid, masked_value)
    row_max = lax.optimization_barrier(jnp.max(score_grid, axis=-1, keepdims=True))
    expo = jnp.exp(score_grid - row_max)
    return (expo / lax.optimization_barrier(jnp.sum(expo, axis=-1, keepdims=True))).astype(jnp.bfloat16)

def reference(history, hist_len, cand_ids, cand_count, table, w_event, w_kv, pool_query, w_rank, w_out):
    score_scale = 1.0 / math.sqrt(HEAD)
    query_heads = pool_query.reshape(PH, HEAD).astype(jnp.float32)
    half_events = HIST // N_SECTION

    def request_step(request):
        events, length, row_ids, live_count = request
        pre_act = jnp.dot(events, w_event, preferred_element_type=jnp.float32)
        states = (events.astype(jnp.float32) + jax.nn.gelu(pre_act)).astype(jnp.bfloat16)
        key_value = jnp.dot(states, w_kv, preferred_element_type=jnp.float32).astype(jnp.bfloat16)
        valid_mask = jnp.arange(HIST) < length
        split_heads = states.reshape(HIST, PH, HEAD).astype(jnp.float32)
        pool_score = jnp.einsum('thc,hc->ht', split_heads, query_heads) * score_scale
        pool_weight = softmax_rows(pool_score, valid_mask[None, :])
        pooled = jnp.einsum('ht,thc->hc', pool_weight.astype(jnp.float32), split_heads)
        user_row = pooled.reshape(D).astype(jnp.bfloat16)
        cand_rows = jnp.take(table, row_ids, axis=0)
        key_part = key_value[:, :E].reshape(HIST, TH, HEAD).astype(jnp.float32)
        value_part = key_value[:, E:].reshape(N_SECTION, half_events, TH, HEAD).astype(jnp.float32)
        target_score = jnp.einsum('jhc,thc->jht', cand_rows.reshape(CAND, TH, HEAD).astype(jnp.float32), key_part) * score_scale
        target_weight = softmax_rows(target_score, valid_mask[None, None, :])
        weight_halves = target_weight.astype(jnp.float32).reshape(CAND, TH, N_SECTION, half_events)
        half_sum = jnp.einsum('jhst,sthc->sjhc', weight_halves, value_part).astype(jnp.bfloat16)
        attended = lax.optimization_barrier(jnp.sum(half_sum.astype(jnp.float32), axis=0)).reshape(CAND, E).astype(jnp.bfloat16)
        pre_rank = jnp.dot(cand_rows, w_rank[:E], preferred_element_type=jnp.float32)
        pre_rank = pre_rank + jnp.dot(attended, w_rank[E:2 * E], preferred_element_type=jnp.float32)
        pre_rank = pre_rank + jnp.dot(user_row[None, :], w_rank[2 * E:], preferred_element_type=jnp.float32)
        rank_hidden = jax.nn.relu(pre_rank)
        cand_score = jnp.dot(rank_hidden, w_out, precision=lax.Precision.HIGHEST)
        cand_score = jnp.where(jnp.arange(CAND) < live_count, cand_score, jnp.zeros_like(cand_score))
        return (cand_score, user_row)
    scores, user_state = lax.map(request_step, (history, hist_len, cand_ids, cand_count))
    return (scores, user_state)
```

```python
import functools
import math

import jax
import jax.numpy as jnp
from jax import lax
from jax.experimental import pallas as pl
from jax.experimental.pallas import tpu as pltpu
from jax.sharding import PartitionSpec as P

MESH = pl.DeviceIdType.MESH
F32 = jnp.float32
BF16 = jnp.bfloat16
I32 = jnp.int32

HEAD = 128
NY, NX, NZ = 4, 4, 8
NYX = NY * NX
CAP = 6
ORDER = (4, 5, 3, 6, 2, 1, 7, 0)
GROUP = 16
NGROUP = NZ * CAP // GROUP
ROWS = 4096
E = 512
D = 1024
HALF = 512
SLOTS = 384
MASKED = -1e30
XY = tuple((dy, dx) for dy in range(NY) for dx in range(NX) if (dy, dx) != (0, 0))


def iota(shape, axis):
    return lax.broadcasted_iota(I32, shape, axis)


def dot(a, b):
    return jnp.dot(a, b, preferred_element_type=F32)


def dot_nt(a, b):
    return lax.dot_general(a, b, (((1,), (1,)), ((), ())), preferred_element_type=F32)


def kernel(
    cap_rows,
    ids_ref, len_ref, count_ref, query_ref, wout_ref,
    history, table, w_event, w_kv, w_rank,
    scores_ref, user_ref,
    hist_v, table_v, we_v, wkv_v, wr_v, states_v, kv_v,
    ids_z, got_z, turn, ids_xy, got_xy, col, pos_row, onehot,
    rows_xy, back_xy, rows_z, back_z, pool_mine, pool_other, bias,
    local_sem, z_send, z_recv, xy_send, xy_recv, rz_send, rz_recv, rxy_send, rxy_recv, pair_send, pair_recv,
):
    section = lax.axis_index("section")
    item = lax.axis_index("item")
    my_y, my_x, my_z = item // (NX * NZ), (item // NZ) % NX, item % NZ
    my_yx = item // NZ

    def load(src, dst, n):
        copy = pltpu.make_async_copy(src, dst, local_sem.at[n])
        copy.start()
        return copy

    load_hist = load(history.at[0], hist_v, 0)
    load_we = load(w_event, we_v, 1)
    load_table = load(table, table_v, 2)
    load_wkv = load(w_kv, wkv_v, 3)
    load_wr = load(w_rank, wr_v, 4)

    def z_peer(plane):
        return (section, my_yx * NZ + plane)

    def xy_index(dy, dx):
        return ((my_y + dy) % NY) * NX + (my_x + dx) % NX

    def xy_peer(yx):
        return (section, yx * NZ + my_z)

    other = (1 - section, item)
    barrier = pltpu.get_barrier_semaphore()
    for dz in range(1, NZ):
        pl.semaphore_signal(barrier, inc=1, device_id=z_peer((my_z + dz) % NZ), device_id_type=MESH)
    for dy, dx in XY:
        pl.semaphore_signal(barrier, inc=1, device_id=xy_peer(xy_index(dy, dx)), device_id_type=MESH)
    pl.semaphore_signal(barrier, inc=1, device_id=other, device_id_type=MESH)

    ids = ids_ref[...]
    owner = lax.shift_right_logical(ids, 12)
    offset = jnp.bitwise_and(ids, ROWS - 1)
    plane = jnp.bitwise_and(owner, NZ - 1)
    yx = lax.shift_right_logical(owner, 3)
    dist = jnp.bitwise_and(my_z - plane + NZ, NZ - 1)
    slot = jnp.zeros_like(dist)
    for s, dz in enumerate(ORDER):
        slot = jnp.where(dist == dz, s, slot)
    owner_hot = iota((NYX * NZ, SLOTS), 0) == owner
    before = (iota((SLOTS, SLOTS), 0) < iota((SLOTS, SLOTS), 1)).astype(F32).astype(BF16)
    earlier = dot(owner_hot.astype(F32).astype(BF16), before)
    rank = jnp.sum(jnp.where(owner_hot, earlier, 0.0), axis=0, keepdims=True).astype(I32)
    place = yx * CAP + rank
    row_of = slot * 8 + rank
    row_hot = (iota((NZ * 8, SLOTS), 0) == row_of).astype(F32).astype(BF16)
    yx_hot = iota((128, SLOTS), 0) == yx

    def spread(value):
        return dot_nt(row_hot, jnp.where(yx_hot, value.astype(F32), 0.0).astype(BF16))

    wanted = offset + 1
    message = (
        spread(jnp.bitwise_and(wanted, 63))
        + 64.0 * spread(lax.shift_right_logical(wanted, 6))
        + 8192.0 * spread(place)
    )
    ids_z[...] = message.reshape(NZ, 8, 128)
    candidate = slot * 128 + place

    pl.semaphore_wait(barrier, NZ - 1 + len(XY) + 1)

    z_ids = []
    for s, dz in enumerate(ORDER):
        if dz:
            z_ids.append(pltpu.make_async_remote_copy(
                src_ref=ids_z.at[s], dst_ref=got_z.at[s], send_sem=z_send.at[s], recv_sem=z_recv.at[s],
                device_id=z_peer((my_z - dz + NZ) % NZ), device_id_type=MESH))
            z_ids[-1].start()
        else:
            got_z[s] = ids_z[s]

    def event_rows(first):
        events = hist_v[first:first + 256, :]
        pre = dot(events, we_v[...])
        states_v[first:first + 256, :] = (events.astype(F32) + jax.nn.gelu(pre)).astype(BF16)

    load_hist.wait()
    load_we.wait()
    event_rows(0)

    for copy in z_ids:
        copy.wait_recv()
    turn[...] = jnp.zeros_like(turn)
    for s in range(NZ):
        turn[s * CAP:(s + 1) * CAP, :] = got_z[s, 0:CAP, :]
    asked = turn[...]
    turned = jnp.transpose(asked)
    for n in range(NYX):
        ids_xy[n] = jnp.broadcast_to(turned[n:n + 1, :], (8, 128))
    xy_ids = []
    for n, (dy, dx) in enumerate(XY):
        target = xy_index(dy, dx)
        xy_ids.append(pltpu.make_async_remote_copy(
            src_ref=ids_xy.at[target], dst_ref=got_xy.at[my_yx], send_sem=xy_send.at[n], recv_sem=xy_recv.at[n],
            device_id=xy_peer(target), device_id_type=MESH))
        xy_ids[-1].start()
    got_xy[my_yx] = ids_xy[my_yx]

    for g in range(NGROUP):
        for n in range(NYX):
            col[n * GROUP:(n + 1) * GROUP, :] = jnp.broadcast_to(
                asked[g * GROUP:(g + 1) * GROUP, n:n + 1], (GROUP, 128))
        pos_row[g] = jnp.transpose(col[...])

    event_rows(256)

    for copy in xy_ids:
        copy.wait_recv()
    turn[...] = jnp.zeros_like(turn)
    for n in range(NYX):
        turn[n:n + 1, :] = got_xy[n, 0:1, :]
    columns = jnp.bitwise_and(jnp.transpose(turn[...]).astype(I32), 8191)
    load_table.wait()

    xy_rows = []
    lanes = iota((1, 128), 1) + 1
    chunk = 1024
    for g in range(NGROUP):
        wants = jnp.concatenate(
            [jnp.broadcast_to(columns[g * GROUP:(g + 1) * GROUP, n:n + 1], (GROUP, 128)) for n in range(NYX)], axis=0)
        total = None
        for first in range(0, ROWS, chunk):
            for block in range(0, chunk, 128):
                onehot[:, block:block + 128] = jnp.where(
                    wants == lanes + (first + block), 1.0, 0.0).astype(BF16)
            term = dot(onehot[...], table_v[first:first + chunk, :])
            total = term if total is None else total + term
        rows_xy[g] = total.astype(BF16).reshape(NYX, GROUP, E)
        for n, (dy, dx) in enumerate(XY):
            target = xy_index(dy, dx)
            xy_rows.append(pltpu.make_async_remote_copy(
                src_ref=rows_xy.at[g, target], dst_ref=back_xy.at[g, my_yx],
                send_sem=rxy_send.at[g, n], recv_sem=rxy_recv.at[g, n],
                device_id=xy_peer(target), device_id_type=MESH))
            xy_rows[-1].start()
        back_xy[g, my_yx] = rows_xy[g, my_yx]

    load_wkv.wait()
    kv_v[section] = dot(states_v[...], wkv_v[...]).astype(BF16)
    kv_copy = pltpu.make_async_remote_copy(
        src_ref=kv_v.at[section], dst_ref=kv_v.at[section], send_sem=pair_send.at[0], recv_sem=pair_recv.at[0],
        device_id=other, device_id_type=MESH)
    kv_copy.start()

    scale = 1.0 / math.sqrt(HEAD)
    length = len_ref[0]
    heads = D // HEAD
    of_head = (iota((16, D), 1) // HEAD) == iota((16, D), 0)
    queries = jnp.where(of_head, query_ref[...].astype(F32), 0.0).astype(BF16)
    events = section * HALF + iota((1, HALF), 1)
    pool_score = jnp.where(events < length, dot_nt(queries, states_v[...]) * scale, MASKED)
    pool_max = jnp.max(pool_score, axis=-1, keepdims=True)
    pool_exp = jnp.exp(pool_score - pool_max)
    pool_sum = jnp.sum(pool_exp, axis=-1, keepdims=True)
    pooled = dot(pool_exp.astype(BF16), states_v[...])

    def by_channel(x):
        return jnp.sum(jnp.where(of_head, x, 0.0), axis=0, keepdims=True)

    pool_mine[...] = jnp.concatenate(
        [by_channel(pooled), by_channel(pool_max), by_channel(pool_sum), jnp.zeros((5, D), F32)], axis=0)
    pool_copy = pltpu.make_async_remote_copy(
        src_ref=pool_mine, dst_ref=pool_other, send_sem=pair_send.at[1], recv_sem=pair_recv.at[1],
        device_id=other, device_id_type=MESH)
    pool_copy.start()

    z_rows = []

    def forward(s):
        total = None
        for g in range(NGROUP):
            if (s + 1) * CAP <= g * GROUP or s * CAP >= (g + 1) * GROUP:
                continue
            entries = pos_row[g][0:cap_rows, :].astype(I32)
            here = jnp.bitwise_and(iota((1, NYX * GROUP), 1), GROUP - 1) + g * GROUP
            mine = (here >= s * CAP) & (here < (s + 1) * CAP)
            filled = jnp.bitwise_and(entries, 8191) > 0
            pick = (lax.shift_right_logical(entries, 13) == iota((cap_rows, NYX * GROUP), 0)) & filled & mine
            term = dot(pick.astype(F32).astype(BF16), back_xy[g].reshape(NYX * GROUP, E))
            total = term if total is None else total + term
        if ORDER[s]:
            rows_z[s] = total.astype(BF16)
            z_rows.append(pltpu.make_async_remote_copy(
                src_ref=rows_z.at[s], dst_ref=back_z.at[s], send_sem=rz_send.at[s], recv_sem=rz_recv.at[s],
                device_id=z_peer((my_z + ORDER[s]) % NZ), device_id_type=MESH))
            z_rows[-1].start()
        else:
            back_z[s] = total.astype(BF16)

    for g in range(NGROUP):
        for copy in xy_rows[g * len(XY):(g + 1) * len(XY)]:
            copy.wait_recv()
        for s in range(NZ):
            if g * GROUP < (s + 1) * CAP <= (g + 1) * GROUP:
                forward(s)

    pool_copy.wait_recv()
    mine, theirs = pool_mine[...], pool_other[...]
    first = jnp.where(section == 0, mine, theirs)
    second = jnp.where(section == 0, theirs, mine)
    joint = jnp.maximum(first[1:2], second[1:2])
    first_scale, second_scale = jnp.exp(first[1:2] - joint), jnp.exp(second[1:2] - joint)
    state = (first[0:1] * first_scale + second[0:1] * second_scale) / (
        first[2:3] * first_scale + second[2:3] * second_scale)
    state = state.astype(BF16)
    user_ref[...] = state
    load_wr.wait()
    user_term = dot(jnp.broadcast_to(state, (16, D)), wr_v[2 * E:, :])[0:1]
    kv_copy.wait_recv()
    bias[...] = jnp.where(iota((8, 2 * HALF), 1) < length, 0.0, MASKED)

    def attend(turn_number, so_far):
        s = (turn_number + NZ - 1) % NZ

        @pl.when(s != NZ - 1)
        def _():
            pltpu.make_async_remote_copy(
                src_ref=rows_z.at[s], dst_ref=back_z.at[s], send_sem=rz_send.at[s], recv_sem=rz_recv.at[s],
                device_id=other, device_id_type=MESH).wait_recv()

        rows = back_z[s]
        parts = []
        for h in range(E // HEAD):
            c = h * HEAD
            keys = kv_v[:, :, c:c + HEAD].reshape(2 * HALF, HEAD)
            score = dot_nt(rows[:, c:c + HEAD], keys) * scale + bias[0:1]
            top = jnp.max(score, axis=-1, keepdims=True)
            expo = jnp.exp(score - top)
            inverse = 1.0 / jnp.sum(expo, axis=-1, keepdims=True)
            weight = (expo * inverse).astype(BF16)
            halves = [
                dot(weight[:, k * HALF:(k + 1) * HALF], kv_v[k, :, E + c:E + c + HEAD]).astype(BF16).astype(F32)
                for k in range(2)]
            parts.append((halves[0] + halves[1]).astype(BF16))
        attended = jnp.concatenate(parts, axis=-1)
        hidden = dot(rows, wr_v[0:E, :]) + dot(attended, wr_v[E:2 * E, :]) + user_term
        score = jnp.sum(jnp.maximum(hidden, 0.0) * wout_ref[...], axis=-1, keepdims=True)
        mine = (iota((cap_rows, SLOTS), 0) + s * 128) == candidate
        return so_far + jnp.sum(jnp.where(mine, score, 0.0), axis=0, keepdims=True)

    found = lax.fori_loop(0, NZ, attend, jnp.zeros((1, SLOTS), F32))
    live = section * SLOTS + iota((1, SLOTS), 1) < count_ref[0]
    scores_ref[...] = jnp.where(live, found, 0.0)

    for copy in z_ids + xy_ids + xy_rows + z_rows + [kv_copy, pool_copy]:
        copy.wait_send()


def fetch_and_rank(cap_rows, collective_id, hist_len, cand_ids, cand_count, pool_query, w_out, history, table,
                   w_event, w_kv, w_rank):
    vmem = pl.BlockSpec(memory_space=pltpu.VMEM)
    smem = pl.BlockSpec(memory_space=pltpu.SMEM)
    anywhere = pl.BlockSpec(memory_space=pl.ANY)
    dma = pltpu.SemaphoreType.DMA
    scratch = [
        pltpu.VMEM((HALF, D), BF16), pltpu.VMEM((ROWS, E), BF16), pltpu.VMEM((D, D), BF16),
        pltpu.VMEM((D, 2 * E), BF16), pltpu.VMEM((2 * E + D, E), BF16), pltpu.VMEM((HALF, D), BF16),
        pltpu.VMEM((2, HALF, 2 * E), BF16),
        pltpu.VMEM((NZ, 8, 128), F32), pltpu.VMEM((NZ, 8, 128), F32), pltpu.VMEM((128, 128), F32),
        pltpu.VMEM((NYX, 8, 128), F32), pltpu.VMEM((NYX, 8, 128), F32),
        pltpu.VMEM((NYX * GROUP, 128), F32), pltpu.VMEM((NGROUP, 128, NYX * GROUP), F32),
        pltpu.VMEM((NYX * GROUP, 1024), BF16),
        pltpu.VMEM((NGROUP, NYX, GROUP, E), BF16), pltpu.VMEM((NGROUP, NYX, GROUP, E), BF16),
        pltpu.VMEM((NZ, cap_rows, E), BF16), pltpu.VMEM((NZ, cap_rows, E), BF16),
        pltpu.VMEM((8, D), F32), pltpu.VMEM((8, D), F32), pltpu.VMEM((8, 2 * HALF), F32),
        dma((5,)), dma((NZ,)), dma((NZ,)), dma((len(XY),)), dma((len(XY),)), dma((NZ,)), dma((NZ,)),
        dma((NGROUP, len(XY))), dma((NGROUP, len(XY))), dma((2,)), dma((2,)),
    ]
    return pl.pallas_call(
        functools.partial(kernel, cap_rows),
        out_shape=(jax.ShapeDtypeStruct((1, SLOTS), F32), jax.ShapeDtypeStruct((1, D), BF16)),
        in_specs=[vmem, smem, smem, vmem, vmem] + [anywhere] * 5,
        out_specs=(vmem, vmem),
        scratch_shapes=scratch,
        compiler_params=pltpu.CompilerParams(
            collective_id=collective_id, has_side_effects=True, vmem_limit_bytes=48 * 1024 * 1024),
        name="fetch_and_rank",
    )(cand_ids, hist_len, cand_count, pool_query.reshape(1, D), w_out.reshape(1, E), history, table, w_event, w_kv,
      w_rank)


def on_device(
    history, hist_len, cand_ids, cand_count, table, w_event, w_kv, pool_query, w_rank, w_out
):
    return fetch_and_rank(
        NYX * CAP, 0, hist_len, cand_ids, cand_count, pool_query, w_out, history, table, w_event, w_kv, w_rank)


def solution(mesh):
    placed = (
        P("item", "section", None),
        P("item"),
        P("item", "section"),
        P("item"),
        P("item", None),
        P(),
        P(),
        P(),
        P(),
        P(),
    )
    return jax.shard_map(
        on_device,
        mesh=mesh,
        in_specs=placed,
        out_specs=(P("item", "section"), P("item", None)),
        check_vma=False,
    )
```

```python
import functools
import math

import jax
import jax.numpy as jnp
from jax import lax
from jax.experimental import pallas as pl
from jax.experimental.pallas import tpu as pltpu
from jax.sharding import PartitionSpec as P

MESH = pl.DeviceIdType.MESH
F32 = jnp.float32
BF16 = jnp.bfloat16
I32 = jnp.int32

HEAD = 128
NY, NX, NZ = 4, 4, 8
NYX = NY * NX
CAP = 6
ORDER = (4, 5, 3, 6, 2, 1, 7, 0)
ROOM = 64
GROUP = 16
NGROUP = NZ * CAP // GROUP
ROWS = 4096
E = 512
D = 1024
HALF = 512
SLOTS = 384
MASKED = -1e30
XY = tuple((dy, dx) for dy in range(NY) for dx in range(NX) if (dy, dx) != (0, 0))


def iota(shape, axis):
    return lax.broadcasted_iota(I32, shape, axis)


def dot(a, b):
    return jnp.dot(a, b, preferred_element_type=F32)


def dot_nt(a, b):
    return lax.dot_general(a, b, (((1,), (1,)), ((), ())), preferred_element_type=F32)


def kernel(
    cap_rows,
    ids_ref, len_ref, count_ref, query_ref, wout_ref,
    history, table, w_event, w_kv, w_rank,
    scores_ref, user_ref, over_ref,
    hist_v, table_v, we_v, wkv_v, wr_v, states_v, kv_v,
    ids_z, got_z, turn, ids_xy, got_xy, col, pos_row, onehot,
    rows_xy, back_xy, rows_z, back_z, pool_mine, pool_other, keys_v, values_v,
    local_sem, z_send, z_recv, xy_send, xy_recv, rz_send, rz_recv, rxy_send, rxy_recv, pair_send, pair_recv,
):
    section = lax.axis_index("section")
    item = lax.axis_index("item")
    my_y, my_x, my_z = item // (NX * NZ), (item // NZ) % NX, item % NZ
    my_yx = item // NZ

    def load(src, dst, n):
        copy = pltpu.make_async_copy(src, dst, local_sem.at[n])
        copy.start()
        return copy

    load_hist = load(history.at[0], hist_v, 0)
    load_we = load(w_event, we_v, 1)
    load_table = load(table, table_v, 2)
    load_wkv = load(w_kv, wkv_v, 3)
    load_wr = load(w_rank, wr_v, 4)

    def z_peer(plane):
        return (section, my_yx * NZ + plane)

    def xy_index(dy, dx):
        return ((my_y + dy) % NY) * NX + (my_x + dx) % NX

    def xy_peer(yx):
        return (section, yx * NZ + my_z)

    other = (1 - section, item)
    barrier = pltpu.get_barrier_semaphore()
    for dz in range(1, NZ):
        pl.semaphore_signal(barrier, inc=1, device_id=z_peer((my_z + dz) % NZ), device_id_type=MESH)
    for dy, dx in XY:
        pl.semaphore_signal(barrier, inc=1, device_id=xy_peer(xy_index(dy, dx)), device_id_type=MESH)
    pl.semaphore_signal(barrier, inc=1, device_id=other, device_id_type=MESH)

    ids = ids_ref[...]
    owner = lax.shift_right_logical(ids, 12)
    offset = jnp.bitwise_and(ids, ROWS - 1)
    plane = jnp.bitwise_and(owner, NZ - 1)
    yx = lax.shift_right_logical(owner, 3)
    dist = jnp.bitwise_and(my_z - plane + NZ, NZ - 1)
    slot = jnp.zeros_like(dist)
    for s, dz in enumerate(ORDER):
        slot = jnp.where(dist == dz, s, slot)
    owner_hot = iota((NYX * NZ, SLOTS), 0) == owner
    before = (iota((SLOTS, SLOTS), 0) < iota((SLOTS, SLOTS), 1)).astype(F32).astype(BF16)
    slot_hot = iota((16, SLOTS), 0) == slot
    hot = jnp.concatenate([owner_hot.astype(F32), slot_hot.astype(F32)], axis=0).astype(BF16)
    earlier = dot(hot, before)
    owners = NYX * NZ
    rank = jnp.sum(jnp.where(owner_hot, earlier[0:owners], 0.0), axis=0, keepdims=True).astype(I32)
    if cap_rows < NYX * CAP:
        place = jnp.sum(jnp.where(slot_hot, earlier[owners:], 0.0), axis=0, keepdims=True).astype(I32)
    else:
        place = yx * CAP + rank
    over = jnp.max(jnp.where(place < cap_rows, 0.0, 1.0), axis=1, keepdims=True)
    row_of = slot * 8 + rank
    row_hot = (iota((NZ * 8, SLOTS), 0) == row_of).astype(F32).astype(BF16)
    yx_hot = iota((128, SLOTS), 0) == yx

    def spread(value):
        return dot_nt(row_hot, jnp.where(yx_hot, value.astype(F32), 0.0).astype(BF16))

    wanted = offset + 1
    message = (
        spread(jnp.bitwise_and(wanted, 63))
        + 64.0 * spread(lax.shift_right_logical(wanted, 6))
        + 8192.0 * spread(place)
    )
    message = message + jnp.where(jnp.bitwise_and(iota((NZ * 8, 128), 0), 7) == CAP, over, 0.0)
    ids_z[...] = message.reshape(NZ, 8, 128)
    candidate = slot * cap_rows + place

    pl.semaphore_wait(barrier, NZ - 1 + len(XY) + 1)

    z_ids = []
    for s, dz in enumerate(ORDER):
        if dz:
            z_ids.append(pltpu.make_async_remote_copy(
                src_ref=ids_z.at[s], dst_ref=got_z.at[s], send_sem=z_send.at[s], recv_sem=z_recv.at[s],
                device_id=z_peer((my_z - dz + NZ) % NZ), device_id_type=MESH))
            z_ids[-1].start()
        else:
            got_z[s] = ids_z[s]

    for copy in z_ids:
        copy.wait_recv()
    turn[...] = jnp.zeros_like(turn)
    for s in range(NZ):
        turn[s * CAP:(s + 1) * CAP, :] = got_z[s, 0:CAP, :]
    asked = turn[...]
    turned = jnp.transpose(asked)
    over = jnp.max(got_z[:, CAP, :], axis=0, keepdims=True)
    for n in range(NYX):
        ids_xy[n] = jnp.where(iota((8, 128), 0) == 0, turned[n:n + 1, :], over)
    xy_ids = []
    for n, (dy, dx) in enumerate(XY):
        target = xy_index(dy, dx)
        xy_ids.append(pltpu.make_async_remote_copy(
            src_ref=ids_xy.at[target], dst_ref=got_xy.at[my_yx], send_sem=xy_send.at[n], recv_sem=xy_recv.at[n],
            device_id=xy_peer(target), device_id_type=MESH))
        xy_ids[-1].start()
    got_xy[my_yx] = ids_xy[my_yx]

    for g in range(NGROUP):
        for n in range(NYX):
            col[n * GROUP:(n + 1) * GROUP, :] = jnp.broadcast_to(
                asked[g * GROUP:(g + 1) * GROUP, n:n + 1], (GROUP, 128))
        pos_row[g] = jnp.transpose(col[...])

    for copy in xy_ids:
        copy.wait_recv()
    turn[...] = jnp.zeros_like(turn)
    for n in range(NYX):
        turn[n:n + 1, :] = got_xy[n, 0:1, :]
    over = jnp.max(got_xy[:, 1, :], axis=0, keepdims=True)
    columns = jnp.bitwise_and(jnp.transpose(turn[...]).astype(I32), 8191)
    load_table.wait()

    xy_rows = []
    lanes = iota((1, 128), 1) + 1
    chunk = 1024
    for g in range(NGROUP):
        wants = jnp.concatenate(
            [jnp.broadcast_to(columns[g * GROUP:(g + 1) * GROUP, n:n + 1], (GROUP, 128)) for n in range(NYX)], axis=0)
        total = None
        for first in range(0, ROWS, chunk):
            for block in range(0, chunk, 128):
                onehot[:, block:block + 128] = jnp.where(
                    wants == lanes + (first + block), 1.0, 0.0).astype(BF16)
            term = dot(onehot[...], table_v[first:first + chunk, :])
            total = term if total is None else total + term
        rows_xy[g] = total.astype(BF16).reshape(NYX, GROUP, E)
        for n, (dy, dx) in enumerate(XY):
            target = xy_index(dy, dx)
            xy_rows.append(pltpu.make_async_remote_copy(
                src_ref=rows_xy.at[g, target], dst_ref=back_xy.at[g, my_yx],
                send_sem=rxy_send.at[g, n], recv_sem=rxy_recv.at[g, n],
                device_id=xy_peer(target), device_id_type=MESH))
            xy_rows[-1].start()
        back_xy[g, my_yx] = rows_xy[g, my_yx]

    load_hist.wait()
    load_we.wait()
    for first in range(0, HALF, 256):
        events = hist_v[first:first + 256, :]
        pre = dot(events, we_v[...])
        states_v[first:first + 256, :] = (events.astype(F32) + jax.nn.gelu(pre)).astype(BF16)

    z_rows = []

    def z_copy(s, src, dst, plane):
        return pltpu.make_async_remote_copy(
            src_ref=src, dst_ref=dst, send_sem=rz_send.at[s], recv_sem=rz_recv.at[s],
            device_id=z_peer(plane), device_id_type=MESH)

    def forward(s):
        total = None
        for g in range(NGROUP):
            if (s + 1) * CAP <= g * GROUP or s * CAP >= (g + 1) * GROUP:
                continue
            entries = pos_row[g][0:cap_rows, :].astype(I32)
            here = jnp.bitwise_and(iota((1, NYX * GROUP), 1), GROUP - 1) + g * GROUP
            mine = (here >= s * CAP) & (here < (s + 1) * CAP)
            filled = jnp.bitwise_and(entries, 8191) > 0
            pick = (lax.shift_right_logical(entries, 13) == iota((cap_rows, NYX * GROUP), 0)) & filled & mine
            term = dot(pick.astype(F32).astype(BF16), back_xy[g].reshape(NYX * GROUP, E))
            total = term if total is None else total + term
        if ORDER[s]:
            rows_z[s] = total.astype(BF16)
            z_rows.append(z_copy(s, rows_z.at[s], back_z.at[s], (my_z + ORDER[s]) % NZ))
            z_rows[-1].start()
        else:
            back_z[s] = total.astype(BF16)

    def forward_group(g):
        for copy in xy_rows[g * len(XY):(g + 1) * len(XY)]:
            copy.wait_recv()
        for s in range(NZ):
            if g * GROUP < (s + 1) * CAP <= (g + 1) * GROUP:
                forward(s)

    forward_group(0)

    load_wkv.wait()
    kv_v[section] = dot(states_v[...], wkv_v[...]).astype(BF16)
    kv_copy = pltpu.make_async_remote_copy(
        src_ref=kv_v.at[section], dst_ref=kv_v.at[section], send_sem=pair_send.at[0], recv_sem=pair_recv.at[0],
        device_id=other, device_id_type=MESH)
    kv_copy.start()

    scale = 1.0 / math.sqrt(HEAD)
    length = len_ref[0]
    of_head = (iota((16, D), 1) // HEAD) == iota((16, D), 0)
    queries = jnp.where(of_head, query_ref[...].astype(F32).reshape(1, D), 0.0).astype(BF16)
    events = section * HALF + iota((1, HALF), 1)
    pool_score = jnp.where(events < length, dot_nt(queries, states_v[...]) * scale, MASKED)
    pool_max = jnp.max(pool_score, axis=-1, keepdims=True)
    pool_exp = jnp.exp(pool_score - pool_max)
    pool_sum = jnp.sum(pool_exp, axis=-1, keepdims=True)
    pooled = dot(pool_exp.astype(BF16), states_v[...])

    def by_channel(x):
        return jnp.sum(jnp.where(of_head, x, 0.0), axis=0, keepdims=True)

    pool_mine[...] = jnp.concatenate(
        [by_channel(pooled), by_channel(pool_max), by_channel(pool_sum)]
        + [jnp.concatenate([over] * (D // 128), axis=1)] * 5, axis=0)
    pool_copy = pltpu.make_async_remote_copy(
        src_ref=pool_mine, dst_ref=pool_other, send_sem=pair_send.at[1], recv_sem=pair_recv.at[1],
        device_id=other, device_id_type=MESH)
    pool_copy.start()

    forward_group(1)
    forward_group(2)

    pool_copy.wait_recv()
    mine, theirs = pool_mine[...], pool_other[...]
    first = jnp.where(section == 0, mine, theirs)
    second = jnp.where(section == 0, theirs, mine)
    joint = jnp.maximum(first[1:2], second[1:2])
    first_scale, second_scale = jnp.exp(first[1:2] - joint), jnp.exp(second[1:2] - joint)
    state = (first[0:1] * first_scale + second[0:1] * second_scale) / (
        first[2:3] * first_scale + second[2:3] * second_scale)
    state = state.astype(BF16)
    user_ref[...] = state
    over_ref[...] = jnp.maximum(mine[3:4, 0:128], theirs[3:4, 0:128])
    load_wr.wait()
    user_term = dot(jnp.broadcast_to(state, (16, D)), wr_v[2 * E:, :])[0:1]
    kv_copy.wait_recv()
    for k in range(2):
        keys_v[:, k * HALF:(k + 1) * HALF] = jnp.transpose(kv_v[k, :, 0:E])
        for h in range(E // HEAD):
            values_v[h, k * HALF:(k + 1) * HALF, 0:HEAD] = kv_v[k, :, E + h * HEAD:E + (h + 1) * HEAD]
            values_v[h, k * HALF:(k + 1) * HALF, HEAD:] = jnp.ones((HALF, HEAD), BF16)
    bias = jnp.where(iota((1, 2 * HALF), 1) < length, 0.0, MASKED)

    pair = 2 * cap_rows

    def attend(step, so_far):
        for s in (2 * step, 2 * step + 1):
            @pl.when(s != NZ - 1)
            def _():
                z_copy(s, rows_z.at[s], back_z.at[s], my_z).wait_recv()

        rows = back_z[pl.ds(2 * step, 2)].reshape(pair, E)

        def scores(h):
            return dot(rows[:, h * HEAD:(h + 1) * HEAD], keys_v[h * HEAD:(h + 1) * HEAD, :])

        heads_total = E // HEAD
        ready = scores(0)
        parts = []
        for h in range(heads_total):
            score = ready * (scale * math.log2(math.e)) + bias
            if h + 1 < heads_total:
                ready = scores(h + 1)
            expo = jnp.exp2(score - jnp.max(score, axis=-1, keepdims=True)).astype(BF16)
            early = dot(expo[:, 0:HALF], values_v[h, 0:HALF, :])
            late = dot(expo[:, HALF:], values_v[h, HALF:, :])
            inverse = 1.0 / (early[:, HEAD:] + late[:, HEAD:])
            early = (early[:, 0:HEAD] * inverse).astype(BF16).astype(F32)
            late = (late[:, 0:HEAD] * inverse).astype(BF16).astype(F32)
            parts.append((early + late).astype(BF16))
        attended = jnp.concatenate(parts, axis=-1)
        hidden = dot(rows, wr_v[0:E, :]) + dot(attended, wr_v[E:2 * E, :]) + user_term
        score = jnp.sum(jnp.maximum(hidden, 0.0) * wout_ref[...], axis=-1, keepdims=True)
        mine = (iota((pair, SLOTS), 0) + step * pair) == candidate
        return so_far + jnp.sum(jnp.where(mine, score, 0.0), axis=0, keepdims=True)

    found = lax.fori_loop(0, NZ // 2, attend, jnp.zeros((1, SLOTS), F32))
    live = section * SLOTS + iota((1, SLOTS), 1) < count_ref[0]
    scores_ref[...] = jnp.where(live, found, 0.0)

    for copy in z_ids + xy_ids + xy_rows + z_rows + [kv_copy, pool_copy]:
        copy.wait_send()


def fetch_and_rank(cap_rows, collective_id, hist_len, cand_ids, cand_count, pool_query, w_out, history, table,
                   w_event, w_kv, w_rank):
    vmem = pl.BlockSpec(memory_space=pltpu.VMEM)
    smem = pl.BlockSpec(memory_space=pltpu.SMEM)
    anywhere = pl.BlockSpec(memory_space=pl.ANY)
    dma = pltpu.SemaphoreType.DMA
    scratch = [
        pltpu.VMEM((HALF, D), BF16), pltpu.VMEM((ROWS, E), BF16), pltpu.VMEM((D, D), BF16),
        pltpu.VMEM((D, 2 * E), BF16), pltpu.VMEM((2 * E + D, E), BF16), pltpu.VMEM((HALF, D), BF16),
        pltpu.VMEM((2, HALF, 2 * E), BF16),
        pltpu.VMEM((NZ, 8, 128), F32), pltpu.VMEM((NZ, 8, 128), F32), pltpu.VMEM((128, 128), F32),
        pltpu.VMEM((NYX, 8, 128), F32), pltpu.VMEM((NYX, 8, 128), F32),
        pltpu.VMEM((NYX * GROUP, 128), F32), pltpu.VMEM((NGROUP, 128, NYX * GROUP), F32),
        pltpu.VMEM((NYX * GROUP, 1024), BF16),
        pltpu.VMEM((NGROUP, NYX, GROUP, E), BF16), pltpu.VMEM((NGROUP, NYX, GROUP, E), BF16),
        pltpu.VMEM((NZ, cap_rows, E), BF16), pltpu.VMEM((NZ, cap_rows, E), BF16),
        pltpu.VMEM((8, D), F32), pltpu.VMEM((8, D), F32),
        pltpu.VMEM((E, 2 * HALF), BF16), pltpu.VMEM((E // HEAD, 2 * HALF, 2 * HEAD), BF16),
        dma((5,)), dma((NZ,)), dma((NZ,)), dma((len(XY),)), dma((len(XY),)), dma((NZ,)), dma((NZ,)),
        dma((NGROUP, len(XY))), dma((NGROUP, len(XY))), dma((2,)), dma((2,)),
    ]
    return pl.pallas_call(
        functools.partial(kernel, cap_rows),
        out_shape=(
            jax.ShapeDtypeStruct((1, SLOTS), F32), jax.ShapeDtypeStruct((1, D), BF16),
            jax.ShapeDtypeStruct((1, 128), F32)),
        in_specs=[vmem, smem, smem, vmem, vmem] + [anywhere] * 5,
        out_specs=(vmem, vmem, vmem),
        scratch_shapes=scratch,
        compiler_params=pltpu.CompilerParams(
            collective_id=collective_id, has_side_effects=True, vmem_limit_bytes=60 * 1024 * 1024),
        name="fetch_and_rank",
    )(cand_ids, hist_len, cand_count, pool_query, w_out.reshape(1, E), history, table, w_event, w_kv,
      w_rank)


def on_device(
    history, hist_len, cand_ids, cand_count, table, w_event, w_kv, pool_query, w_rank, w_out
):
    operands = (hist_len, cand_ids, cand_count, pool_query, w_out, history, table, w_event, w_kv, w_rank)
    scores, user_state, over = fetch_and_rank(ROOM, 0, *operands)
    scores = lax.cond(
        over[0, 0] > 0.0, lambda: fetch_and_rank(NYX * CAP, 1, *operands)[0], lambda: scores)
    return scores, user_state


def solution(mesh):
    placed = (
        P("item", "section", None),
        P("item"),
        P("item", "section"),
        P("item"),
        P("item", None),
        P(),
        P(),
        P(),
        P(),
        P(),
    )
    return jax.shard_map(
        on_device,
        mesh=mesh,
        in_specs=placed,
        out_specs=(P("item", "section"), P("item", None)),
        check_vma=False,
    )
```

```python
import functools
import math

import jax
import jax.numpy as jnp
from jax import lax
from jax.experimental import pallas as pl
from jax.experimental.pallas import tpu as pltpu
from jax.sharding import PartitionSpec as P

MESH = pl.DeviceIdType.MESH
F32 = jnp.float32
BF16 = jnp.bfloat16
I32 = jnp.int32

HEAD = 128
NY, NX, NZ = 4, 4, 8
NYX = NY * NX
CAP = 6
ORDER = (4, 5, 3, 6, 2, 1, 7, 0)
ROOM = 56
GROUP = 16
NGROUP = NZ * CAP // GROUP
ROWS = 4096
E = 512
D = 1024
HALF = 512
SLOTS = 384
MASKED = -1e30
XY = tuple((dy, dx) for dy in range(NY) for dx in range(NX) if (dy, dx) != (0, 0))


def iota(shape, axis):
    return lax.broadcasted_iota(I32, shape, axis)


def dot(a, b):
    return jnp.dot(a, b, preferred_element_type=F32)


def dot_nt(a, b):
    return lax.dot_general(a, b, (((1,), (1,)), ((), ())), preferred_element_type=F32)


def kernel(
    cap_rows,
    len_ref, count_ref, cand_ids, pool_query, w_out,
    history, table, w_event, w_kv, w_rank,
    scores_ref, user_ref, over_ref,
    ids_v, query_v, wout_v, user_v, over_v, hist_v, table_v, we_v, wkv_v, wr_v, states_v, kv_v,
    ids_z, got_z, turn, ids_xy, got_xy, col, pos_row, onehot,
    rows_xy, back_xy, rows_z, back_z, pool_mine, pool_other, keys_v, values_v,
    local_sem, z_send, z_recv, xy_send, xy_recv, rz_send, rz_recv, rxy_send, rxy_recv, pair_send, pair_recv,
):
    section = lax.axis_index("section")
    item = lax.axis_index("item")
    my_y, my_x, my_z = item // (NX * NZ), (item // NZ) % NX, item % NZ
    my_yx = item // NZ

    def load(src, dst, n):
        copy = pltpu.make_async_copy(src, dst, local_sem.at[n])
        copy.start()
        return copy

    load_ids = load(cand_ids, ids_v, 5)

    def drain(block, sem):
        pltpu.make_async_copy(block, block, sem).wait()


    def z_peer(plane):
        return (section, my_yx * NZ + plane)

    def xy_index(dy, dx):
        return ((my_y + dy) % NY) * NX + (my_x + dx) % NX

    def xy_peer(yx):
        return (section, yx * NZ + my_z)

    other = (1 - section, item)
    barrier = pltpu.get_barrier_semaphore()
    for dz in range(1, NZ):
        pl.semaphore_signal(barrier, inc=1, device_id=z_peer((my_z + dz) % NZ), device_id_type=MESH)
    for dy, dx in XY:
        pl.semaphore_signal(barrier, inc=1, device_id=xy_peer(xy_index(dy, dx)), device_id_type=MESH)
    pl.semaphore_signal(barrier, inc=1, device_id=other, device_id_type=MESH)

    load_hist = load(history.at[0], hist_v, 0)
    load_we = load(w_event, we_v, 1)
    load_table = load(table, table_v, 2)
    load_wkv = load(w_kv, wkv_v, 3)
    load_wr = load(w_rank, wr_v, 4)
    load_query = load(pool_query, query_v, 6)
    load_wout = load(w_out, wout_v, 7)

    load_ids.wait()
    ids = ids_v[...]
    owner = lax.shift_right_logical(ids, 12)
    offset = jnp.bitwise_and(ids, ROWS - 1)
    plane = jnp.bitwise_and(owner, NZ - 1)
    yx = lax.shift_right_logical(owner, 3)
    dist = jnp.bitwise_and(my_z - plane + NZ, NZ - 1)
    slot = jnp.zeros_like(dist)
    for s, dz in enumerate(ORDER):
        slot = jnp.where(dist == dz, s, slot)
    owner_hot = iota((NYX * NZ, SLOTS), 0) == owner
    before = (iota((SLOTS, SLOTS), 0) < iota((SLOTS, SLOTS), 1)).astype(F32).astype(BF16)
    slot_hot = iota((16, SLOTS), 0) == slot
    hot = jnp.concatenate([owner_hot.astype(F32), slot_hot.astype(F32)], axis=0).astype(BF16)
    earlier = dot(hot, before)
    owners = NYX * NZ
    rank = jnp.sum(jnp.where(owner_hot, earlier[0:owners], 0.0), axis=0, keepdims=True).astype(I32)
    if cap_rows < NYX * CAP:
        place = jnp.sum(jnp.where(slot_hot, earlier[owners:], 0.0), axis=0, keepdims=True).astype(I32)
    else:
        place = yx * CAP + rank
    over = jnp.max(jnp.where(place < cap_rows, 0.0, 1.0), axis=1, keepdims=True)
    row_of = slot * 8 + rank
    row_hot = (iota((NZ * 8, SLOTS), 0) == row_of).astype(F32).astype(BF16)
    yx_hot = iota((128, SLOTS), 0) == yx

    def spread(value):
        return dot_nt(row_hot, jnp.where(yx_hot, value.astype(F32), 0.0).astype(BF16))

    wanted = offset + 1
    message = (
        spread(jnp.bitwise_and(wanted, 63))
        + 64.0 * spread(lax.shift_right_logical(wanted, 6))
        + 8192.0 * spread(place)
    )
    message = message + jnp.where(jnp.bitwise_and(iota((NZ * 8, 128), 0), 7) == CAP, over, 0.0)
    ids_z[...] = message.reshape(NZ, 8, 128)
    candidate = slot * cap_rows + place

    pl.semaphore_wait(barrier, NZ - 1 + len(XY) + 1)

    for s, dz in enumerate(ORDER):
        if dz:
            pltpu.make_async_remote_copy(
                src_ref=ids_z.at[s], dst_ref=got_z.at[s], send_sem=z_send, recv_sem=z_recv,
                device_id=z_peer((my_z - dz + NZ) % NZ), device_id_type=MESH).start()
        else:
            got_z[s] = ids_z[s]

    def event_rows(first):
        rows = pl.ds(first, HALF // 2)
        pre = dot(hist_v[rows, :], we_v[...])
        states_v[rows, :] = (hist_v[rows, :].astype(F32) + jax.nn.gelu(pre)).astype(BF16)

    load_hist.wait()
    load_we.wait()
    event_rows(0)

    drain(got_z.at[pl.ds(0, NZ - 1)], z_recv)
    turn[...] = jnp.zeros_like(turn)
    for s in range(NZ):
        turn[s * CAP:(s + 1) * CAP, :] = got_z[s, 0:CAP, :]
    asked = turn[...]
    turned = jnp.transpose(asked)
    over = jnp.max(got_z[:, CAP, :], axis=0, keepdims=True)
    for n in range(NYX):
        ids_xy[n] = jnp.where(iota((8, 128), 0) == 0, turned[n:n + 1, :], over)
    for dy, dx in XY:
        target = xy_index(dy, dx)
        pltpu.make_async_remote_copy(
            src_ref=ids_xy.at[target], dst_ref=got_xy.at[my_yx], send_sem=xy_send, recv_sem=xy_recv,
            device_id=xy_peer(target), device_id_type=MESH).start()
    got_xy[my_yx] = ids_xy[my_yx]

    for g in range(NGROUP):
        for n in range(NYX):
            col[n * GROUP:(n + 1) * GROUP, :] = jnp.broadcast_to(
                asked[g * GROUP:(g + 1) * GROUP, n:n + 1], (GROUP, 128))
        pos_row[g] = jnp.transpose(col[...])

    event_rows(HALF // 2)

    drain(got_xy.at[pl.ds(0, NYX - 1)], xy_recv)
    turn[...] = jnp.zeros_like(turn)
    for n in range(NYX):
        turn[n:n + 1, :] = got_xy[n, 0:1, :]
    over = jnp.max(got_xy[:, 1, :], axis=0, keepdims=True)
    columns = jnp.bitwise_and(jnp.transpose(turn[...]).astype(I32), 8191)
    load_table.wait()

    lanes = iota((1, 128), 1) + 1
    chunk = 1024
    for g in range(NGROUP):
        wants = jnp.concatenate(
            [jnp.broadcast_to(columns[g * GROUP:(g + 1) * GROUP, n:n + 1], (GROUP, 128)) for n in range(NYX)], axis=0)
        total = None
        for first in range(0, ROWS, chunk):
            for block in range(0, chunk, 128):
                onehot[:, block:block + 128] = jnp.where(
                    wants == lanes + (first + block), 1.0, 0.0).astype(BF16)
            term = dot(onehot[...], table_v[first:first + chunk, :])
            total = term if total is None else total + term
        rows_xy[g] = total.astype(BF16).reshape(NYX, GROUP, E)
        for dy, dx in XY:
            target = xy_index(dy, dx)
            pltpu.make_async_remote_copy(
                src_ref=rows_xy.at[g, target], dst_ref=back_xy.at[g, my_yx],
                send_sem=rxy_send, recv_sem=rxy_recv.at[g],
                device_id=xy_peer(target), device_id_type=MESH).start()
        back_xy[g, my_yx] = rows_xy[g, my_yx]

    def z_copy(s, src, dst, plane):
        return pltpu.make_async_remote_copy(
            src_ref=src, dst_ref=dst, send_sem=rz_send, recv_sem=rz_recv.at[s],
            device_id=z_peer(plane), device_id_type=MESH)

    def forward(s):
        total = None
        for g in range(NGROUP):
            if (s + 1) * CAP <= g * GROUP or s * CAP >= (g + 1) * GROUP:
                continue
            entries = pos_row[g][0:cap_rows, :].astype(I32)
            here = jnp.bitwise_and(iota((1, NYX * GROUP), 1), GROUP - 1) + g * GROUP
            mine = (here >= s * CAP) & (here < (s + 1) * CAP)
            filled = jnp.bitwise_and(entries, 8191) > 0
            pick = (lax.shift_right_logical(entries, 13) == iota((cap_rows, NYX * GROUP), 0)) & filled & mine
            term = dot(pick.astype(F32).astype(BF16), back_xy[g].reshape(NYX * GROUP, E))
            total = term if total is None else total + term
        if ORDER[s]:
            rows_z[s] = total.astype(BF16)
            z_copy(s, rows_z.at[s], back_z.at[s], (my_z + ORDER[s]) % NZ).start()
        else:
            back_z[s] = total.astype(BF16)

    def forward_group(g):
        drain(back_xy.at[g, pl.ds(0, NYX - 1)], rxy_recv.at[g])
        for s in range(NZ):
            if g * GROUP < (s + 1) * CAP <= (g + 1) * GROUP:
                forward(s)

    forward_group(0)

    load_wkv.wait()
    kv_v[section] = dot(states_v[...], wkv_v[...]).astype(BF16)
    kv_copy = pltpu.make_async_remote_copy(
        src_ref=kv_v.at[section], dst_ref=kv_v.at[section], send_sem=pair_send.at[0], recv_sem=pair_recv.at[0],
        device_id=other, device_id_type=MESH)
    kv_copy.start()

    load_query.wait()
    scale = 1.0 / math.sqrt(HEAD)
    length = len_ref[0]
    of_head = (iota((16, D), 1) // HEAD) == iota((16, D), 0)
    queries = jnp.where(of_head, query_v[...].astype(F32).reshape(1, D), 0.0).astype(BF16)
    events = section * HALF + iota((1, HALF), 1)
    pool_score = jnp.where(events < length, dot_nt(queries, states_v[...]) * scale, MASKED)
    pool_max = jnp.max(pool_score, axis=-1, keepdims=True)
    pool_exp = jnp.exp(pool_score - pool_max)
    pool_sum = jnp.sum(pool_exp, axis=-1, keepdims=True)
    pooled = dot(pool_exp.astype(BF16), states_v[...])

    def by_channel(x):
        return jnp.sum(jnp.where(of_head, x, 0.0), axis=0, keepdims=True)

    pool_mine[...] = jnp.concatenate(
        [by_channel(pooled), by_channel(pool_max), by_channel(pool_sum)]
        + [jnp.concatenate([over] * (D // 128), axis=1)] * 5, axis=0)
    pool_copy = pltpu.make_async_remote_copy(
        src_ref=pool_mine, dst_ref=pool_other, send_sem=pair_send.at[1], recv_sem=pair_recv.at[1],
        device_id=other, device_id_type=MESH)
    pool_copy.start()

    forward_group(1)

    pool_copy.wait_recv()
    mine, theirs = pool_mine[...], pool_other[...]
    first = jnp.where(section == 0, mine, theirs)
    second = jnp.where(section == 0, theirs, mine)
    joint = jnp.maximum(first[1:2], second[1:2])
    first_scale, second_scale = jnp.exp(first[1:2] - joint), jnp.exp(second[1:2] - joint)
    state = (first[0:1] * first_scale + second[0:1] * second_scale) / (
        first[2:3] * first_scale + second[2:3] * second_scale)
    state = state.astype(BF16)
    user_v[...] = state
    over_v[...] = jnp.maximum(mine[3:4, 0:128], theirs[3:4, 0:128])
    put_user = load(user_v, user_ref, 8)
    put_over = load(over_v, over_ref, 9)
    load_wr.wait()
    load_wout.wait()
    user_term = dot(jnp.broadcast_to(state, (16, D)), wr_v[2 * E:, :])[0:1]
    kv_copy.wait_recv()
    for k in range(2):
        keys_v[:, k * HALF:(k + 1) * HALF] = jnp.transpose(kv_v[k, :, 0:E])
        for h in range(E // HEAD):
            values_v[h, k * HALF:(k + 1) * HALF, 0:HEAD] = kv_v[k, :, E + h * HEAD:E + (h + 1) * HEAD]
            values_v[h, k * HALF:(k + 1) * HALF, HEAD:] = jnp.ones((HALF, HEAD), BF16)
    bias = jnp.where(iota((1, 2 * HALF), 1) < length, 0.0, MASKED)

    forward_group(2)

    pair = 2 * cap_rows

    def attend(step, so_far):
        for s in (2 * step, 2 * step + 1):
            @pl.when(s != NZ - 1)
            def _():
                z_copy(s, rows_z.at[s], back_z.at[s], my_z).wait_recv()

        rows = back_z[pl.ds(2 * step, 2)].reshape(pair, E)

        def scores(h):
            return dot(rows[:, h * HEAD:(h + 1) * HEAD], keys_v[h * HEAD:(h + 1) * HEAD, :])

        heads_total = E // HEAD
        ready = scores(0)
        parts = []
        for h in range(heads_total):
            score = ready * (scale * math.log2(math.e)) + bias
            if h + 1 < heads_total:
                ready = scores(h + 1)
            expo = jnp.exp2(score - jnp.max(score, axis=-1, keepdims=True)).astype(BF16)
            early = dot(expo[:, 0:HALF], values_v[h, 0:HALF, :])
            late = dot(expo[:, HALF:], values_v[h, HALF:, :])
            inverse = 1.0 / (early[:, HEAD:] + late[:, HEAD:])
            early = (early[:, 0:HEAD] * inverse).astype(BF16).astype(F32)
            late = (late[:, 0:HEAD] * inverse).astype(BF16).astype(F32)
            parts.append((early + late).astype(BF16))
        attended = jnp.concatenate(parts, axis=-1)
        hidden = dot(rows, wr_v[0:E, :]) + dot(attended, wr_v[E:2 * E, :]) + user_term
        score = jnp.sum(jnp.maximum(hidden, 0.0) * wout_v[...].reshape(1, E), axis=-1, keepdims=True)
        mine = (iota((pair, SLOTS), 0) + step * pair) == candidate
        return so_far + jnp.sum(jnp.where(mine, score, 0.0), axis=0, keepdims=True)

    found = lax.fori_loop(0, NZ // 2, attend, jnp.zeros((1, SLOTS), F32))
    live = section * SLOTS + iota((1, SLOTS), 1) < count_ref[0]
    scores_ref[...] = jnp.where(live, found, 0.0)

    drain(ids_z.at[pl.ds(0, NZ - 1)], z_send)
    drain(ids_xy.at[pl.ds(0, NYX - 1)], xy_send)
    drain(rows_xy.at[:, pl.ds(0, NYX - 1)], rxy_send)
    drain(rows_z.at[pl.ds(0, NZ - 1)], rz_send)
    kv_copy.wait_send()
    pool_copy.wait_send()
    put_user.wait()
    put_over.wait()


def fetch_and_rank(cap_rows, collective_id, hist_len, cand_ids, cand_count, pool_query, w_out, history, table,
                   w_event, w_kv, w_rank):
    vmem = pl.BlockSpec(memory_space=pltpu.VMEM)
    smem = pl.BlockSpec(memory_space=pltpu.SMEM)
    anywhere = pl.BlockSpec(memory_space=pl.ANY)
    dma = pltpu.SemaphoreType.DMA
    scratch = [
        pltpu.VMEM((1, SLOTS), I32), pltpu.VMEM((D,), BF16), pltpu.VMEM((E,), F32),
        pltpu.VMEM((1, D), BF16), pltpu.VMEM((1, 128), F32),
        pltpu.VMEM((HALF, D), BF16), pltpu.VMEM((ROWS, E), BF16), pltpu.VMEM((D, D), BF16),
        pltpu.VMEM((D, 2 * E), BF16), pltpu.VMEM((2 * E + D, E), BF16), pltpu.VMEM((HALF, D), BF16),
        pltpu.VMEM((2, HALF, 2 * E), BF16),
        pltpu.VMEM((NZ, 8, 128), F32), pltpu.VMEM((NZ, 8, 128), F32), pltpu.VMEM((128, 128), F32),
        pltpu.VMEM((NYX, 8, 128), F32), pltpu.VMEM((NYX, 8, 128), F32),
        pltpu.VMEM((NYX * GROUP, 128), F32), pltpu.VMEM((NGROUP, 128, NYX * GROUP), F32),
        pltpu.VMEM((NYX * GROUP, 1024), BF16),
        pltpu.VMEM((NGROUP, NYX, GROUP, E), BF16), pltpu.VMEM((NGROUP, NYX, GROUP, E), BF16),
        pltpu.VMEM((NZ, cap_rows, E), BF16), pltpu.VMEM((NZ, cap_rows, E), BF16),
        pltpu.VMEM((8, D), F32), pltpu.VMEM((8, D), F32),
        pltpu.VMEM((E, 2 * HALF), BF16), pltpu.VMEM((E // HEAD, 2 * HALF, 2 * HEAD), BF16),
        dma((10,)), dma, dma, dma, dma, dma, dma((NZ,)), dma, dma((NGROUP,)), dma((2,)), dma((2,)),
    ]
    return pl.pallas_call(
        functools.partial(kernel, cap_rows),
        out_shape=(
            jax.ShapeDtypeStruct((1, SLOTS), F32), jax.ShapeDtypeStruct((1, D), BF16),
            jax.ShapeDtypeStruct((1, 128), F32)),
        in_specs=[smem, smem] + [anywhere] * 8,
        out_specs=(vmem, anywhere, anywhere),
        scratch_shapes=scratch,
        compiler_params=pltpu.CompilerParams(
            collective_id=collective_id, has_side_effects=True, vmem_limit_bytes=60 * 1024 * 1024),
        name="fetch_and_rank",
    )(hist_len, cand_count, cand_ids, pool_query, w_out, history, table, w_event, w_kv, w_rank)


def on_device(
    history, hist_len, cand_ids, cand_count, table, w_event, w_kv, pool_query, w_rank, w_out
):
    operands = (hist_len, cand_ids, cand_count, pool_query, w_out, history, table, w_event, w_kv, w_rank)
    scores, user_state, over = fetch_and_rank(ROOM, 0, *operands)
    scores = lax.cond(
        over[0, 0] > 0.0, lambda: fetch_and_rank(NYX * CAP, 1, *operands)[0], lambda: scores)
    return scores, user_state


def solution(mesh):
    placed = (
        P("item", "section", None),
        P("item"),
        P("item", "section"),
        P("item"),
        P("item", None),
        P(),
        P(),
        P(),
        P(),
        P(),
    )
    return jax.shard_map(
        on_device,
        mesh=mesh,
        in_specs=placed,
        out_specs=(P("item", "section"), P("item", None)),
        check_vma=False,
    )
```

```python
import functools
import math

import jax
import jax.numpy as jnp
from jax import lax
from jax.experimental import pallas as pl
from jax.experimental.pallas import tpu as pltpu
from jax.sharding import PartitionSpec as P

MESH = pl.DeviceIdType.MESH
F32 = jnp.float32
BF16 = jnp.bfloat16
I32 = jnp.int32

HEAD = 128
NY, NX, NZ = 4, 4, 8
NYX = NY * NX
CAP = 6
ORDER = (4, 5, 3, 6, 2, 1, 7, 0)
ROOM = 56
GROUPS = (8, 16, 24)
STARTS = tuple(sum(GROUPS[:g]) for g in range(len(GROUPS)))
ROWS = 4096
E = 512
D = 1024
HALF = 512
SLOTS = 384
MASKED = -1e30
XY = tuple((dy, dx) for dy in (2, 1, 3, 0) for dx in (2, 1, 3, 0) if (dy, dx) != (0, 0))


def iota(shape, axis):
    return lax.broadcasted_iota(I32, shape, axis)


def dot(a, b):
    return jnp.dot(a, b, preferred_element_type=F32)


def dot_nt(a, b):
    return lax.dot_general(a, b, (((1,), (1,)), ((), ())), preferred_element_type=F32)


def kernel(
    cap_rows,
    len_ref, count_ref, cand_ids, pool_query, w_out,
    history, table, w_event, w_kv, w_rank,
    scores_ref, user_ref, over_ref,
    ids_v, query_v, wout_v, user_v, over_v, hist_v, table_v, we_v, wkv_v, wr_v, states_v, kv_v,
    ids_z, got_z, turn, ids_xy, got_xy, col, pos_rows, onehot,
    rows_xy, back_xy, rows_z, back_z, pool_mine, pool_other, keys_v, values_v,
    local_sem, z_send, z_recv, xy_send, xy_recv, rz_send, rz_recv, rxy_send, rxy_recv, pair_send, pair_recv,
):
    section = lax.axis_index("section")
    item = lax.axis_index("item")
    my_y, my_x, my_z = item // (NX * NZ), (item // NZ) % NX, item % NZ
    my_yx = item // NZ

    def load(src, dst, n):
        copy = pltpu.make_async_copy(src, dst, local_sem.at[n])
        copy.start()
        return copy

    load_ids = load(cand_ids, ids_v, 5)

    def drain(block, sem):
        pltpu.make_async_copy(block, block, sem).wait()


    def z_peer(plane):
        return (section, my_yx * NZ + plane)

    def xy_index(dy, dx):
        return ((my_y + dy) % NY) * NX + (my_x + dx) % NX

    def xy_peer(yx):
        return (section, yx * NZ + my_z)

    other = (1 - section, item)
    barrier = pltpu.get_barrier_semaphore()
    for dz in range(1, NZ):
        pl.semaphore_signal(barrier, inc=1, device_id=z_peer((my_z + dz) % NZ), device_id_type=MESH)
    for dy, dx in XY:
        pl.semaphore_signal(barrier, inc=1, device_id=xy_peer(xy_index(dy, dx)), device_id_type=MESH)
    pl.semaphore_signal(barrier, inc=1, device_id=other, device_id_type=MESH)

    load_hist = load(history.at[0], hist_v, 0)
    load_we = load(w_event, we_v, 1)
    load_table = load(table, table_v, 2)
    load_wkv = load(w_kv, wkv_v, 3)
    load_wr = load(w_rank, wr_v, 4)
    load_query = load(pool_query, query_v, 6)
    load_wout = load(w_out, wout_v, 7)

    load_ids.wait()
    ids = ids_v[...]
    owner = lax.shift_right_logical(ids, 12)
    offset = jnp.bitwise_and(ids, ROWS - 1)
    plane = jnp.bitwise_and(owner, NZ - 1)
    yx = lax.shift_right_logical(owner, 3)
    dist = jnp.bitwise_and(my_z - plane + NZ, NZ - 1)
    slot = jnp.zeros_like(dist)
    for s, dz in enumerate(ORDER):
        slot = jnp.where(dist == dz, s, slot)
    owner_hot = iota((NYX * NZ, SLOTS), 0) == owner
    before = (iota((SLOTS, SLOTS), 0) < iota((SLOTS, SLOTS), 1)).astype(F32).astype(BF16)
    slot_hot = iota((16, SLOTS), 0) == slot
    hot = jnp.concatenate([owner_hot.astype(F32), slot_hot.astype(F32)], axis=0).astype(BF16)
    earlier = dot(hot, before)
    owners = NYX * NZ
    rank = jnp.sum(jnp.where(owner_hot, earlier[0:owners], 0.0), axis=0, keepdims=True).astype(I32)
    if cap_rows < NYX * CAP:
        place = jnp.sum(jnp.where(slot_hot, earlier[owners:], 0.0), axis=0, keepdims=True).astype(I32)
    else:
        place = yx * CAP + rank
    over = jnp.max(jnp.where(place < cap_rows, 0.0, 1.0), axis=1, keepdims=True)
    row_of = slot * 8 + rank
    row_hot = (iota((NZ * 8, SLOTS), 0) == row_of).astype(F32).astype(BF16)
    yx_hot = iota((128, SLOTS), 0) == yx

    def spread(value):
        return dot_nt(row_hot, jnp.where(yx_hot, value.astype(F32), 0.0).astype(BF16))

    wanted = offset + 1
    message = (
        spread(jnp.bitwise_and(wanted, 63))
        + 64.0 * spread(lax.shift_right_logical(wanted, 6))
        + 8192.0 * spread(place)
    )
    message = message + jnp.where(jnp.bitwise_and(iota((NZ * 8, 128), 0), 7) == CAP, over, 0.0)
    ids_z[...] = message.reshape(NZ, 8, 128)
    candidate = slot * cap_rows + place

    pl.semaphore_wait(barrier, NZ - 1 + len(XY) + 1)

    for s, dz in enumerate(ORDER):
        if dz:
            pltpu.make_async_remote_copy(
                src_ref=ids_z.at[s], dst_ref=got_z.at[s], send_sem=z_send, recv_sem=z_recv,
                device_id=z_peer((my_z - dz + NZ) % NZ), device_id_type=MESH).start()
        else:
            got_z[s] = ids_z[s]

    def event_rows(first):
        rows = pl.ds(first, HALF // 2)
        pre = dot(hist_v[rows, :], we_v[...])
        states_v[rows, :] = (hist_v[rows, :].astype(F32) + jax.nn.gelu(pre)).astype(BF16)

    load_hist.wait()
    load_we.wait()
    event_rows(0)

    drain(got_z.at[pl.ds(0, NZ - 1)], z_recv)
    turn[...] = jnp.zeros_like(turn)
    for s in range(NZ):
        turn[s * CAP:(s + 1) * CAP, :] = got_z[s, 0:CAP, :]
    asked = turn[...]
    turned = jnp.transpose(asked)
    over = jnp.max(got_z[:, CAP, :], axis=0, keepdims=True)
    for n in range(NYX):
        ids_xy[n] = jnp.where(iota((8, 128), 0) == 0, turned[n:n + 1, :], over)
    for dy, dx in XY:
        target = xy_index(dy, dx)
        pltpu.make_async_remote_copy(
            src_ref=ids_xy.at[target], dst_ref=got_xy.at[my_yx], send_sem=xy_send, recv_sem=xy_recv,
            device_id=xy_peer(target), device_id_type=MESH).start()
    got_xy[my_yx] = ids_xy[my_yx]

    for size, start, pos_row in zip(GROUPS, STARTS, pos_rows):
        for n in range(NYX):
            col[n * size:(n + 1) * size, :] = jnp.broadcast_to(asked[start:start + size, n:n + 1], (size, 128))
        pos_row[...] = jnp.transpose(col[0:NYX * size, :])

    event_rows(HALF // 2)

    drain(got_xy.at[pl.ds(0, NYX - 1)], xy_recv)
    turn[...] = jnp.zeros_like(turn)
    for n in range(NYX):
        turn[n:n + 1, :] = got_xy[n, 0:1, :]
    over = jnp.max(got_xy[:, 1, :], axis=0, keepdims=True)
    columns = jnp.bitwise_and(jnp.transpose(turn[...]).astype(I32), 8191)
    load_table.wait()

    lanes = iota((1, 128), 1) + 1
    chunk = 1024
    for g, (size, start) in enumerate(zip(GROUPS, STARTS)):
        count = NYX * size
        wants = jnp.concatenate(
            [jnp.broadcast_to(columns[start:start + size, n:n + 1], (size, 128)) for n in range(NYX)], axis=0)
        total = None
        for first in range(0, ROWS, chunk):
            for block in range(0, chunk, 128):
                onehot[0:count, block:block + 128] = jnp.where(
                    wants == lanes + (first + block), 1.0, 0.0).astype(BF16)
            term = dot(onehot[0:count, :], table_v[first:first + chunk, :])
            total = term if total is None else total + term
        rows_xy[g][...] = total.astype(BF16).reshape(NYX, size, E)
        for dy, dx in XY:
            target = xy_index(dy, dx)
            pltpu.make_async_remote_copy(
                src_ref=rows_xy[g].at[target], dst_ref=back_xy[g].at[my_yx],
                send_sem=rxy_send.at[g], recv_sem=rxy_recv.at[g],
                device_id=xy_peer(target), device_id_type=MESH).start()
        back_xy[g][my_yx] = rows_xy[g][my_yx]

    def z_copy(s, src, dst, plane):
        return pltpu.make_async_remote_copy(
            src_ref=src, dst_ref=dst, send_sem=rz_send, recv_sem=rz_recv.at[s],
            device_id=z_peer(plane), device_id_type=MESH)

    def forward(s):
        total = None
        for g, (size, start) in enumerate(zip(GROUPS, STARTS)):
            if (s + 1) * CAP <= start or s * CAP >= start + size:
                continue
            entries = pos_rows[g][0:cap_rows, :].astype(I32)
            here = lax.rem(iota((1, NYX * size), 1), size) + start
            mine = (here >= s * CAP) & (here < (s + 1) * CAP)
            filled = jnp.bitwise_and(entries, 8191) > 0
            pick = (lax.shift_right_logical(entries, 13) == iota((cap_rows, NYX * size), 0)) & filled & mine
            term = dot(pick.astype(F32).astype(BF16), back_xy[g][...].reshape(NYX * size, E))
            total = term if total is None else total + term
        if ORDER[s]:
            rows_z[s] = total.astype(BF16)
            z_copy(s, rows_z.at[s], back_z.at[s], (my_z + ORDER[s]) % NZ).start()
        else:
            back_z[s] = total.astype(BF16)

    def forward_group(g):
        drain(back_xy[g].at[pl.ds(0, NYX - 1)], rxy_recv.at[g])
        for s in range(NZ):
            if STARTS[g] < (s + 1) * CAP <= STARTS[g] + GROUPS[g]:
                forward(s)

    forward_group(0)

    load_wkv.wait()
    kv_v[section] = dot(states_v[...], wkv_v[...]).astype(BF16)
    kv_copy = pltpu.make_async_remote_copy(
        src_ref=kv_v.at[section], dst_ref=kv_v.at[section], send_sem=pair_send.at[0], recv_sem=pair_recv.at[0],
        device_id=other, device_id_type=MESH)
    kv_copy.start()

    load_query.wait()
    scale = 1.0 / math.sqrt(HEAD)
    length = len_ref[0]
    of_head = (iota((16, D), 1) // HEAD) == iota((16, D), 0)
    queries = jnp.where(of_head, query_v[...].astype(F32).reshape(1, D), 0.0).astype(BF16)
    events = section * HALF + iota((1, HALF), 1)
    pool_score = jnp.where(events < length, dot_nt(queries, states_v[...]) * scale, MASKED)
    pool_max = jnp.max(pool_score, axis=-1, keepdims=True)
    pool_exp = jnp.exp(pool_score - pool_max)
    pool_sum = jnp.sum(pool_exp, axis=-1, keepdims=True)
    pooled = dot(pool_exp.astype(BF16), states_v[...])

    def by_channel(x):
        return jnp.sum(jnp.where(of_head, x, 0.0), axis=0, keepdims=True)

    pool_mine[...] = jnp.concatenate(
        [by_channel(pooled), by_channel(pool_max), by_channel(pool_sum)]
        + [jnp.concatenate([over] * (D // 128), axis=1)] * 5, axis=0)
    pool_copy = pltpu.make_async_remote_copy(
        src_ref=pool_mine, dst_ref=pool_other, send_sem=pair_send.at[1], recv_sem=pair_recv.at[1],
        device_id=other, device_id_type=MESH)
    pool_copy.start()

    forward_group(1)

    pool_copy.wait_recv()
    mine, theirs = pool_mine[...], pool_other[...]
    first = jnp.where(section == 0, mine, theirs)
    second = jnp.where(section == 0, theirs, mine)
    joint = jnp.maximum(first[1:2], second[1:2])
    first_scale, second_scale = jnp.exp(first[1:2] - joint), jnp.exp(second[1:2] - joint)
    state = (first[0:1] * first_scale + second[0:1] * second_scale) / (
        first[2:3] * first_scale + second[2:3] * second_scale)
    state = state.astype(BF16)
    user_v[...] = state
    over_v[...] = jnp.maximum(mine[3:4, 0:128], theirs[3:4, 0:128])
    put_user = load(user_v, user_ref, 8)
    put_over = load(over_v, over_ref, 9)
    load_wr.wait()
    load_wout.wait()
    user_term = dot(jnp.broadcast_to(state, (16, D)), wr_v[2 * E:, :])[0:1]
    kv_copy.wait_recv()
    for k in range(2):
        keys_v[:, k * HALF:(k + 1) * HALF] = jnp.transpose(kv_v[k, :, 0:E])
        for h in range(E // HEAD):
            values_v[h, k * HALF:(k + 1) * HALF, 0:HEAD] = kv_v[k, :, E + h * HEAD:E + (h + 1) * HEAD]
            values_v[h, k * HALF:(k + 1) * HALF, HEAD:] = jnp.ones((HALF, HEAD), BF16)
    bias = jnp.where(iota((1, 2 * HALF), 1) < length, 0.0, MASKED)

    forward_group(2)

    batch = 4 * cap_rows

    def attend(step, so_far):
        for s in (4 * step, 4 * step + 1, 4 * step + 2, 4 * step + 3):
            @pl.when(s != NZ - 1)
            def _():
                z_copy(s, rows_z.at[s], back_z.at[s], my_z).wait_recv()

        rows = back_z[pl.ds(4 * step, 4)].reshape(batch, E)

        def scores(h):
            return dot(rows[:, h * HEAD:(h + 1) * HEAD], keys_v[h * HEAD:(h + 1) * HEAD, :])

        heads_total = E // HEAD
        ready = scores(0)
        parts = []
        for h in range(heads_total):
            score = ready * (scale * math.log2(math.e)) + bias
            if h + 1 < heads_total:
                ready = scores(h + 1)
            expo = jnp.exp2(score - jnp.max(score, axis=-1, keepdims=True)).astype(BF16)
            early = dot(expo[:, 0:HALF], values_v[h, 0:HALF, :])
            late = dot(expo[:, HALF:], values_v[h, HALF:, :])
            inverse = 1.0 / (early[:, HEAD:] + late[:, HEAD:])
            early = (early[:, 0:HEAD] * inverse).astype(BF16).astype(F32)
            late = (late[:, 0:HEAD] * inverse).astype(BF16).astype(F32)
            parts.append((early + late).astype(BF16))
        attended = jnp.concatenate(parts, axis=-1)
        hidden = dot(rows, wr_v[0:E, :]) + dot(attended, wr_v[E:2 * E, :]) + user_term
        score = jnp.sum(jnp.maximum(hidden, 0.0) * wout_v[...].reshape(1, E), axis=-1, keepdims=True)
        mine = (iota((batch, SLOTS), 0) + step * batch) == candidate
        return so_far + jnp.sum(jnp.where(mine, score, 0.0), axis=0, keepdims=True)

    found = lax.fori_loop(0, NZ // 4, attend, jnp.zeros((1, SLOTS), F32))
    live = section * SLOTS + iota((1, SLOTS), 1) < count_ref[0]
    scores_ref[...] = jnp.where(live, found, 0.0)

    drain(ids_z.at[pl.ds(0, NZ - 1)], z_send)
    drain(ids_xy.at[pl.ds(0, NYX - 1)], xy_send)
    for g in range(len(GROUPS)):
        drain(rows_xy[g].at[pl.ds(0, NYX - 1)], rxy_send.at[g])
    drain(rows_z.at[pl.ds(0, NZ - 1)], rz_send)
    kv_copy.wait_send()
    pool_copy.wait_send()
    put_user.wait()
    put_over.wait()


def fetch_and_rank(cap_rows, collective_id, hist_len, cand_ids, cand_count, pool_query, w_out, history, table,
                   w_event, w_kv, w_rank):
    vmem = pl.BlockSpec(memory_space=pltpu.VMEM)
    smem = pl.BlockSpec(memory_space=pltpu.SMEM)
    anywhere = pl.BlockSpec(memory_space=pl.ANY)
    dma = pltpu.SemaphoreType.DMA
    scratch = [
        pltpu.VMEM((1, SLOTS), I32), pltpu.VMEM((D,), BF16), pltpu.VMEM((E,), F32),
        pltpu.VMEM((1, D), BF16), pltpu.VMEM((1, 128), F32),
        pltpu.VMEM((HALF, D), BF16), pltpu.VMEM((ROWS, E), BF16), pltpu.VMEM((D, D), BF16),
        pltpu.VMEM((D, 2 * E), BF16), pltpu.VMEM((2 * E + D, E), BF16), pltpu.VMEM((HALF, D), BF16),
        pltpu.VMEM((2, HALF, 2 * E), BF16),
        pltpu.VMEM((NZ, 8, 128), F32), pltpu.VMEM((NZ, 8, 128), F32), pltpu.VMEM((128, 128), F32),
        pltpu.VMEM((NYX, 8, 128), F32), pltpu.VMEM((NYX, 8, 128), F32),
        pltpu.VMEM((NYX * max(GROUPS), 128), F32),
        [pltpu.VMEM((128, NYX * size), F32) for size in GROUPS],
        pltpu.VMEM((NYX * max(GROUPS), 1024), BF16),
        [pltpu.VMEM((NYX, size, E), BF16) for size in GROUPS], [pltpu.VMEM((NYX, size, E), BF16) for size in GROUPS],
        pltpu.VMEM((NZ, cap_rows, E), BF16), pltpu.VMEM((NZ, cap_rows, E), BF16),
        pltpu.VMEM((8, D), F32), pltpu.VMEM((8, D), F32),
        pltpu.VMEM((E, 2 * HALF), BF16), pltpu.VMEM((E // HEAD, 2 * HALF, 2 * HEAD), BF16),
        dma((10,)), dma, dma, dma, dma, dma, dma((NZ,)),
        dma((len(GROUPS),)), dma((len(GROUPS),)), dma((2,)), dma((2,)),
    ]
    return pl.pallas_call(
        functools.partial(kernel, cap_rows),
        out_shape=(
            jax.ShapeDtypeStruct((1, SLOTS), F32), jax.ShapeDtypeStruct((1, D), BF16),
            jax.ShapeDtypeStruct((1, 128), F32)),
        in_specs=[smem, smem] + [anywhere] * 8,
        out_specs=(vmem, anywhere, anywhere),
        scratch_shapes=scratch,
        compiler_params=pltpu.CompilerParams(
            collective_id=collective_id, has_side_effects=True, vmem_limit_bytes=60 * 1024 * 1024),
        name="fetch_and_rank",
    )(hist_len, cand_count, cand_ids, pool_query, w_out, history, table, w_event, w_kv, w_rank)


def on_device(
    history, hist_len, cand_ids, cand_count, table, w_event, w_kv, pool_query, w_rank, w_out
):
    operands = (hist_len, cand_ids, cand_count, pool_query, w_out, history, table, w_event, w_kv, w_rank)
    scores, user_state, over = fetch_and_rank(ROOM, 0, *operands)
    scores = lax.cond(
        over[0, 0] > 0.0, lambda: fetch_and_rank(NYX * CAP, 1, *operands)[0], lambda: scores)
    return scores, user_state


def solution(mesh):
    placed = (
        P("item", "section", None),
        P("item"),
        P("item", "section"),
        P("item"),
        P("item", None),
        P(),
        P(),
        P(),
        P(),
        P(),
    )
    return jax.shard_map(
        on_device,
        mesh=mesh,
        in_specs=placed,
        out_specs=(P("item", "section"), P("item", None)),
        check_vma=False,
    )
```

```python
import functools
import math

import jax
import jax.numpy as jnp
from jax import lax
from jax.experimental import pallas as pl
from jax.experimental.pallas import tpu as pltpu
from jax.sharding import PartitionSpec as P

MESH = pl.DeviceIdType.MESH
F32 = jnp.float32
BF16 = jnp.bfloat16
I32 = jnp.int32

HEAD = 128
NY, NX, NZ = 4, 4, 8
NYX = NY * NX
CAP = 6
ORDER = (4, 5, 3, 6, 2, 1, 7, 0)
ROOM = 56
GROUPS = (8, 16, 24)
STARTS = tuple(sum(GROUPS[:g]) for g in range(len(GROUPS)))
ROWS = 4096
E = 512
D = 1024
HALF = 512
SLOTS = 384
MASKED = -1e30
XY = tuple((dy, dx) for dy in (2, 1, 3, 0) for dx in (2, 1, 3, 0) if (dy, dx) != (0, 0))


def iota(shape, axis):
    return lax.broadcasted_iota(I32, shape, axis)


def dot(a, b):
    return jnp.dot(a, b, preferred_element_type=F32)


def dot_nt(a, b):
    return lax.dot_general(a, b, (((1,), (1,)), ((), ())), preferred_element_type=F32)


def kernel(
    cap_rows,
    len_ref, count_ref, cand_ids, pool_query, w_out,
    history, table, w_event, w_kv, w_rank,
    scores_ref, user_ref, over_ref,
    ids_v, query_v, wout_v, user_v, over_v, hist_v, table_v, we_v, wkv_v, wr_v, states_v, kv_v,
    ids_z, got_z, turn, ids_xy, got_xy, col, pos_rows, onehot,
    rows_xy, back_xy, rows_z, back_z, pool_mine, pool_other, keys_v, values_v,
    local_sem, z_send, z_recv, xy_send, xy_recv, rz_send, rz_recv, rxy_send, rxy_recv, pair_send, pair_recv,
):
    section = lax.axis_index("section")
    item = lax.axis_index("item")
    my_y, my_x, my_z = item // (NX * NZ), (item // NZ) % NX, item % NZ
    my_yx = item // NZ

    def load(src, dst, n):
        copy = pltpu.make_async_copy(src, dst, local_sem.at[n])
        copy.start()
        return copy

    load_ids = load(cand_ids, ids_v, 5)

    def drain(block, sem):
        pltpu.make_async_copy(block, block, sem).wait()


    def z_peer(plane):
        return (section, my_yx * NZ + plane)

    def xy_index(dy, dx):
        return ((my_y + dy) % NY) * NX + (my_x + dx) % NX

    def xy_peer(yx):
        return (section, yx * NZ + my_z)

    other = (1 - section, item)
    peers = [xy_index(dy, dx) for dy, dx in XY]
    barrier = pltpu.get_barrier_semaphore()
    for dz in range(1, NZ):
        pl.semaphore_signal(barrier, inc=1, device_id=z_peer((my_z + dz) % NZ), device_id_type=MESH)
    for target in peers:
        pl.semaphore_signal(barrier, inc=1, device_id=xy_peer(target), device_id_type=MESH)
    pl.semaphore_signal(barrier, inc=1, device_id=other, device_id_type=MESH)

    load_hist = load(history.at[0], hist_v, 0)
    load_we = load(w_event, we_v, 1)
    load_table = load(table, table_v, 2)
    load_wkv = load(w_kv, wkv_v, 3)
    load_wr = load(w_rank, wr_v, 4)
    load_query = load(pool_query, query_v, 6)
    load_wout = load(w_out, wout_v, 7)

    load_ids.wait()
    ids = ids_v[...]
    owner = lax.shift_right_logical(ids, 12)
    offset = jnp.bitwise_and(ids, ROWS - 1)
    plane = jnp.bitwise_and(owner, NZ - 1)
    yx = lax.shift_right_logical(owner, 3)
    dist = jnp.bitwise_and(my_z - plane + NZ, NZ - 1)
    slot = jnp.zeros_like(dist)
    for s, dz in enumerate(ORDER):
        slot = jnp.where(dist == dz, s, slot)
    owner_hot = iota((NYX * NZ, SLOTS), 0) == owner
    before = (iota((SLOTS, SLOTS), 0) < iota((SLOTS, SLOTS), 1)).astype(F32).astype(BF16)
    slot_hot = iota((16, SLOTS), 0) == slot
    hot = jnp.concatenate([owner_hot.astype(F32), slot_hot.astype(F32)], axis=0).astype(BF16)
    earlier = dot(hot, before)
    owners = NYX * NZ
    rank = jnp.sum(jnp.where(owner_hot, earlier[0:owners], 0.0), axis=0, keepdims=True).astype(I32)
    if cap_rows < NYX * CAP:
        place = jnp.sum(jnp.where(slot_hot, earlier[owners:], 0.0), axis=0, keepdims=True).astype(I32)
    else:
        place = yx * CAP + rank
    over = jnp.max(jnp.where(place < cap_rows, 0.0, 1.0), axis=1, keepdims=True)
    row_of = slot * 8 + rank
    row_hot = (iota((NZ * 8, SLOTS), 0) == row_of).astype(F32).astype(BF16)
    yx_hot = iota((128, SLOTS), 0) == yx

    def spread(value):
        return dot_nt(row_hot, jnp.where(yx_hot, value.astype(F32), 0.0).astype(BF16))

    wanted = offset + 1
    message = (
        spread(jnp.bitwise_and(wanted, 63))
        + 64.0 * spread(lax.shift_right_logical(wanted, 6))
        + 8192.0 * spread(place)
    )
    message = message + jnp.where(jnp.bitwise_and(iota((NZ * 8, 128), 0), 7) == CAP, over, 0.0)
    ids_z[...] = message.reshape(NZ, 8, 128)
    candidate = slot * cap_rows + place

    pl.semaphore_wait(barrier, NZ - 1 + len(XY) + 1)

    for s, dz in enumerate(ORDER):
        if dz:
            pltpu.make_async_remote_copy(
                src_ref=ids_z.at[s], dst_ref=got_z.at[s], send_sem=z_send, recv_sem=z_recv,
                device_id=z_peer((my_z - dz + NZ) % NZ), device_id_type=MESH).start()
        else:
            got_z[s] = ids_z[s]

    def event_rows(first):
        rows = pl.ds(first, HALF // 2)
        pre = dot(hist_v[rows, :], we_v[...])
        states_v[rows, :] = (hist_v[rows, :].astype(F32) + jax.nn.gelu(pre)).astype(BF16)

    drain(got_z.at[pl.ds(0, NZ - 1)], z_recv)
    turn[...] = jnp.zeros_like(turn)
    for s in range(NZ):
        turn[s * CAP:(s + 1) * CAP, :] = got_z[s, 0:CAP, :]
    asked = turn[...]
    turned = jnp.transpose(asked)
    over = jnp.max(got_z[:, CAP, :], axis=0, keepdims=True)
    for n in range(NYX):
        ids_xy[n] = jnp.where(iota((8, 128), 0) == 0, turned[n:n + 1, :], over)
    for target in peers:
        pltpu.make_async_remote_copy(
            src_ref=ids_xy.at[target], dst_ref=got_xy.at[my_yx], send_sem=xy_send, recv_sem=xy_recv,
            device_id=xy_peer(target), device_id_type=MESH).start()
    got_xy[my_yx] = ids_xy[my_yx]

    for size, start, pos_row in zip(GROUPS, STARTS, pos_rows):
        for n in range(NYX):
            col[n * size:(n + 1) * size, :] = jnp.broadcast_to(asked[start:start + size, n:n + 1], (size, 128))
        pos_row[...] = jnp.transpose(col[0:NYX * size, :])

    load_hist.wait()
    load_we.wait()
    event_rows(0)
    event_rows(HALF // 2)

    drain(got_xy.at[pl.ds(0, NYX - 1)], xy_recv)
    turn[...] = jnp.zeros_like(turn)
    for n in range(NYX):
        turn[n:n + 1, :] = got_xy[n, 0:1, :]
    over = jnp.max(got_xy[:, 1, :], axis=0, keepdims=True)
    columns = jnp.bitwise_and(jnp.transpose(turn[...]).astype(I32), 8191)
    load_table.wait()

    lanes = iota((1, 128), 1) + 1
    chunk = 512
    for g, (size, start) in enumerate(zip(GROUPS, STARTS)):
        count = NYX * size
        wants = jnp.concatenate(
            [jnp.broadcast_to(columns[start:start + size, n:n + 1], (size, 128)) for n in range(NYX)], axis=0)
        total = None
        for first in range(0, ROWS, chunk):
            for block in range(0, chunk, 128):
                onehot[first // chunk, 0:count, block:block + 128] = jnp.where(
                    wants == lanes + (first + block), 1.0, 0.0).astype(BF16)
            term = dot(onehot[first // chunk, 0:count, :], table_v[first:first + chunk, :])
            total = term if total is None else total + term
        rows_xy[g][...] = total.astype(BF16).reshape(NYX, size, E)
        for target in peers:
            pltpu.make_async_remote_copy(
                src_ref=rows_xy[g].at[target], dst_ref=back_xy[g].at[my_yx],
                send_sem=rxy_send.at[g], recv_sem=rxy_recv.at[g],
                device_id=xy_peer(target), device_id_type=MESH).start()
        back_xy[g][my_yx] = rows_xy[g][my_yx]

    def z_copy(s, src, dst, plane):
        return pltpu.make_async_remote_copy(
            src_ref=src, dst_ref=dst, send_sem=rz_send, recv_sem=rz_recv.at[s],
            device_id=z_peer(plane), device_id_type=MESH)

    def forward(s):
        total = None
        for g, (size, start) in enumerate(zip(GROUPS, STARTS)):
            if (s + 1) * CAP <= start or s * CAP >= start + size:
                continue
            entries = pos_rows[g][0:cap_rows, :].astype(I32)
            here = lax.rem(iota((1, NYX * size), 1), size) + start
            mine = (here >= s * CAP) & (here < (s + 1) * CAP)
            filled = jnp.bitwise_and(entries, 8191) > 0
            pick = (lax.shift_right_logical(entries, 13) == iota((cap_rows, NYX * size), 0)) & filled & mine
            term = dot(pick.astype(F32).astype(BF16), back_xy[g][...].reshape(NYX * size, E))
            total = term if total is None else total + term
        if ORDER[s]:
            rows_z[s] = total.astype(BF16)
            z_copy(s, rows_z.at[s], back_z.at[s], (my_z + ORDER[s]) % NZ).start()
        else:
            back_z[s] = total.astype(BF16)

    def forward_group(g):
        drain(back_xy[g].at[pl.ds(0, NYX - 1)], rxy_recv.at[g])
        for s in range(NZ):
            if STARTS[g] < (s + 1) * CAP <= STARTS[g] + GROUPS[g]:
                forward(s)

    forward_group(0)

    load_wkv.wait()
    kv_v[section] = dot(states_v[...], wkv_v[...]).astype(BF16)
    kv_copy = pltpu.make_async_remote_copy(
        src_ref=kv_v.at[section], dst_ref=kv_v.at[section], send_sem=pair_send.at[0], recv_sem=pair_recv.at[0],
        device_id=other, device_id_type=MESH)
    kv_copy.start()

    load_query.wait()
    scale = 1.0 / math.sqrt(HEAD)
    length = len_ref[0]
    of_head = (iota((16, D), 1) // HEAD) == iota((16, D), 0)
    queries = jnp.where(of_head, query_v[...].astype(F32).reshape(1, D), 0.0).astype(BF16)
    events = section * HALF + iota((1, HALF), 1)
    pool_score = jnp.where(events < length, dot_nt(queries, states_v[...]) * scale, MASKED)
    pool_max = jnp.max(pool_score, axis=-1, keepdims=True)
    pool_exp = jnp.exp(pool_score - pool_max)
    pool_sum = jnp.sum(pool_exp, axis=-1, keepdims=True)
    pooled = dot(pool_exp.astype(BF16), states_v[...])

    def by_channel(x):
        return jnp.sum(jnp.where(of_head, x, 0.0), axis=0, keepdims=True)

    pool_mine[...] = jnp.concatenate(
        [by_channel(pooled), by_channel(pool_max), by_channel(pool_sum)]
        + [jnp.concatenate([over] * (D // 128), axis=1)] * 5, axis=0)
    pool_copy = pltpu.make_async_remote_copy(
        src_ref=pool_mine, dst_ref=pool_other, send_sem=pair_send.at[1], recv_sem=pair_recv.at[1],
        device_id=other, device_id_type=MESH)
    pool_copy.start()

    forward_group(1)

    pool_copy.wait_recv()
    mine, theirs = pool_mine[...], pool_other[...]
    first = jnp.where(section == 0, mine, theirs)
    second = jnp.where(section == 0, theirs, mine)
    joint = jnp.maximum(first[1:2], second[1:2])
    first_scale, second_scale = jnp.exp(first[1:2] - joint), jnp.exp(second[1:2] - joint)
    state = (first[0:1] * first_scale + second[0:1] * second_scale) / (
        first[2:3] * first_scale + second[2:3] * second_scale)
    state = state.astype(BF16)
    user_v[...] = state
    over_v[...] = jnp.maximum(mine[3:4, 0:128], theirs[3:4, 0:128])
    put_user = load(user_v, user_ref, 8)
    put_over = load(over_v, over_ref, 9)
    load_wr.wait()
    load_wout.wait()
    user_term = dot(jnp.broadcast_to(state, (16, D)), wr_v[2 * E:, :])[0:1]
    kv_copy.wait_recv()
    for k in range(2):
        keys_v[:, k * HALF:(k + 1) * HALF] = jnp.transpose(kv_v[k, :, 0:E])
        for h in range(E // HEAD):
            values_v[h, k * HALF:(k + 1) * HALF, 0:HEAD] = kv_v[k, :, E + h * HEAD:E + (h + 1) * HEAD]
            values_v[h, k * HALF:(k + 1) * HALF, HEAD:] = jnp.ones((HALF, HEAD), BF16)
    bias = jnp.where(iota((1, 2 * HALF), 1) < length, 0.0, MASKED)

    forward_group(2)

    batch = 4 * cap_rows

    def attend(step, so_far):
        for s in (4 * step, 4 * step + 1, 4 * step + 2, 4 * step + 3):
            @pl.when(s != NZ - 1)
            def _():
                z_copy(s, rows_z.at[s], back_z.at[s], my_z).wait_recv()

        rows = back_z[pl.ds(4 * step, 4)].reshape(batch, E)

        def scores(h):
            return dot(rows[:, h * HEAD:(h + 1) * HEAD], keys_v[h * HEAD:(h + 1) * HEAD, :])

        heads_total = E // HEAD
        ready = scores(0)
        parts = []
        for h in range(heads_total):
            score = ready * (scale * math.log2(math.e)) + bias
            if h + 1 < heads_total:
                ready = scores(h + 1)
            expo = jnp.exp2(score - jnp.max(score, axis=-1, keepdims=True)).astype(BF16)
            early = dot(expo[:, 0:HALF], values_v[h, 0:HALF, :])
            late = dot(expo[:, HALF:], values_v[h, HALF:, :])
            inverse = 1.0 / (early[:, HEAD:] + late[:, HEAD:])
            early = (early[:, 0:HEAD] * inverse).astype(BF16).astype(F32)
            late = (late[:, 0:HEAD] * inverse).astype(BF16).astype(F32)
            parts.append((early + late).astype(BF16))
        attended = jnp.concatenate(parts, axis=-1)
        hidden = dot(rows, wr_v[0:E, :]) + dot(attended, wr_v[E:2 * E, :]) + user_term
        score = jnp.sum(jnp.maximum(hidden, 0.0) * wout_v[...].reshape(1, E), axis=-1, keepdims=True)
        mine = (iota((batch, SLOTS), 0) + step * batch) == candidate
        return so_far + jnp.sum(jnp.where(mine, score, 0.0), axis=0, keepdims=True)

    found = lax.fori_loop(0, NZ // 4, attend, jnp.zeros((1, SLOTS), F32))
    live = section * SLOTS + iota((1, SLOTS), 1) < count_ref[0]
    scores_ref[...] = jnp.where(live, found, 0.0)

    drain(ids_z.at[pl.ds(0, NZ - 1)], z_send)
    drain(ids_xy.at[pl.ds(0, NYX - 1)], xy_send)
    for g in range(len(GROUPS)):
        drain(rows_xy[g].at[pl.ds(0, NYX - 1)], rxy_send.at[g])
    drain(rows_z.at[pl.ds(0, NZ - 1)], rz_send)
    kv_copy.wait_send()
    pool_copy.wait_send()
    put_user.wait()
    put_over.wait()


def fetch_and_rank(cap_rows, collective_id, hist_len, cand_ids, cand_count, pool_query, w_out, history, table,
                   w_event, w_kv, w_rank):
    vmem = pl.BlockSpec(memory_space=pltpu.VMEM)
    smem = pl.BlockSpec(memory_space=pltpu.SMEM)
    anywhere = pl.BlockSpec(memory_space=pl.ANY)
    dma = pltpu.SemaphoreType.DMA
    scratch = [
        pltpu.VMEM((1, SLOTS), I32), pltpu.VMEM((D,), BF16), pltpu.VMEM((E,), F32),
        pltpu.VMEM((1, D), BF16), pltpu.VMEM((1, 128), F32),
        pltpu.VMEM((HALF, D), BF16), pltpu.VMEM((ROWS, E), BF16), pltpu.VMEM((D, D), BF16),
        pltpu.VMEM((D, 2 * E), BF16), pltpu.VMEM((2 * E + D, E), BF16), pltpu.VMEM((HALF, D), BF16),
        pltpu.VMEM((2, HALF, 2 * E), BF16),
        pltpu.VMEM((NZ, 8, 128), F32), pltpu.VMEM((NZ, 8, 128), F32), pltpu.VMEM((128, 128), F32),
        pltpu.VMEM((NYX, 8, 128), F32), pltpu.VMEM((NYX, 8, 128), F32),
        pltpu.VMEM((NYX * max(GROUPS), 128), F32),
        [pltpu.VMEM((128, NYX * size), F32) for size in GROUPS],
        pltpu.VMEM((ROWS // 512, NYX * max(GROUPS), 512), BF16),
        [pltpu.VMEM((NYX, size, E), BF16) for size in GROUPS], [pltpu.VMEM((NYX, size, E), BF16) for size in GROUPS],
        pltpu.VMEM((NZ, cap_rows, E), BF16), pltpu.VMEM((NZ, cap_rows, E), BF16),
        pltpu.VMEM((8, D), F32), pltpu.VMEM((8, D), F32),
        pltpu.VMEM((E, 2 * HALF), BF16), pltpu.VMEM((E // HEAD, 2 * HALF, 2 * HEAD), BF16),
        dma((10,)), dma, dma, dma, dma, dma, dma((NZ,)),
        dma((len(GROUPS),)), dma((len(GROUPS),)), dma((2,)), dma((2,)),
    ]
    return pl.pallas_call(
        functools.partial(kernel, cap_rows),
        out_shape=(
            jax.ShapeDtypeStruct((1, SLOTS), F32), jax.ShapeDtypeStruct((1, D), BF16),
            jax.ShapeDtypeStruct((1, 128), F32)),
        in_specs=[smem, smem] + [anywhere] * 8,
        out_specs=(vmem, anywhere, anywhere),
        scratch_shapes=scratch,
        compiler_params=pltpu.CompilerParams(
            collective_id=collective_id, has_side_effects=True, vmem_limit_bytes=60 * 1024 * 1024),
        name="fetch_and_rank",
    )(hist_len, cand_count, cand_ids, pool_query, w_out, history, table, w_event, w_kv, w_rank)


def on_device(
    history, hist_len, cand_ids, cand_count, table, w_event, w_kv, pool_query, w_rank, w_out
):
    operands = (hist_len, cand_ids, cand_count, pool_query, w_out, history, table, w_event, w_kv, w_rank)
    scores, user_state, over = fetch_and_rank(ROOM, 0, *operands)
    scores = lax.cond(
        over[0, 0] > 0.0, lambda: fetch_and_rank(NYX * CAP, 1, *operands)[0], lambda: scores)
    return scores, user_state


def solution(mesh):
    placed = (
        P("item", "section", None),
        P("item"),
        P("item", "section"),
        P("item"),
        P("item", None),
        P(),
        P(),
        P(),
        P(),
        P(),
    )
    return jax.shard_map(
        on_device,
        mesh=mesh,
        in_specs=placed,
        out_specs=(P("item", "section"), P("item", None)),
        check_vma=False,
    )
```

```python
import functools
import math

import jax
import jax.numpy as jnp
from jax import lax
from jax.experimental import pallas as pl
from jax.experimental.pallas import tpu as pltpu
from jax.sharding import PartitionSpec as P

MESH = pl.DeviceIdType.MESH
F32 = jnp.float32
BF16 = jnp.bfloat16
I32 = jnp.int32

HEAD = 128
NY, NX, NZ = 4, 4, 8
NYX = NY * NX
CAP = 6
ORDER = (4, 5, 3, 6, 2, 1, 7, 0)
ROOM = 56
GROUPS = (8, 16, 24)
STARTS = tuple(sum(GROUPS[:g]) for g in range(len(GROUPS)))
ROWS = 4096
E = 512
D = 1024
HALF = 512
SLOTS = 384
MASKED = -1e30
XY = tuple((dy, dx) for dy in (2, 1, 3, 0) for dx in (2, 1, 3, 0) if (dy, dx) != (0, 0))


def iota(shape, axis):
    return lax.broadcasted_iota(I32, shape, axis)


def dot(a, b):
    return jnp.dot(a, b, preferred_element_type=F32)


def dot_nt(a, b):
    return lax.dot_general(a, b, (((1,), (1,)), ((), ())), preferred_element_type=F32)


def kernel(
    cap_rows,
    len_ref, count_ref, cand_ids, pool_query, w_out,
    history, table, w_event, w_kv, w_rank,
    scores_ref, user_ref, over_ref,
    ids_v, query_v, wout_v, user_v, over_v, hist_v, table_v, we_v, wkv_v, wr_v, states_v, kv_v,
    ids_z, got_z, turn, ids_xy, got_xy, col, pos_rows, onehot,
    rows_xy, back_xy, rows_z, back_z, pool_mine, pool_other, keys_v, values_v,
    local_sem, z_send, z_recv, xy_send, xy_recv, rz_send, rz_recv, rxy_send, rxy_recv, pair_send, pair_recv,
):
    section = lax.axis_index("section")
    item = lax.axis_index("item")
    my_y, my_x, my_z = item // (NX * NZ), (item // NZ) % NX, item % NZ
    my_yx = item // NZ

    def load(src, dst, n):
        copy = pltpu.make_async_copy(src, dst, local_sem.at[n])
        copy.start()
        return copy

    load_ids = load(cand_ids, ids_v, 5)

    def drain(block, sem):
        pltpu.make_async_copy(block, block, sem).wait()


    def z_peer(plane):
        return (section, my_yx * NZ + plane)

    def xy_index(dy, dx):
        return ((my_y + dy) % NY) * NX + (my_x + dx) % NX

    def xy_peer(yx):
        return (section, yx * NZ + my_z)

    other = (1 - section, item)
    peers = [xy_index(dy, dx) for dy, dx in XY]
    barrier = pltpu.get_barrier_semaphore()
    for dz in range(1, NZ):
        pl.semaphore_signal(barrier, inc=1, device_id=z_peer((my_z + dz) % NZ), device_id_type=MESH)
    for target in peers:
        pl.semaphore_signal(barrier, inc=1, device_id=xy_peer(target), device_id_type=MESH)
    pl.semaphore_signal(barrier, inc=1, device_id=other, device_id_type=MESH)

    load_hist = load(history.at[0], hist_v, 0)
    load_we = load(w_event, we_v, 1)
    load_table = load(table, table_v, 2)
    load_wkv = load(w_kv, wkv_v, 3)
    load_wr = load(w_rank, wr_v, 4)
    load_query = load(pool_query, query_v, 6)
    load_wout = load(w_out, wout_v, 7)

    load_ids.wait()
    ids = ids_v[...]
    owner = lax.shift_right_logical(ids, 12)
    offset = jnp.bitwise_and(ids, ROWS - 1)
    plane = jnp.bitwise_and(owner, NZ - 1)
    yx = lax.shift_right_logical(owner, 3)
    dist = jnp.bitwise_and(my_z - plane + NZ, NZ - 1)
    slot = jnp.zeros_like(dist)
    for s, dz in enumerate(ORDER):
        slot = jnp.where(dist == dz, s, slot)
    owner_hot = iota((NYX * NZ, SLOTS), 0) == owner
    before = (iota((SLOTS, SLOTS), 0) < iota((SLOTS, SLOTS), 1)).astype(F32).astype(BF16)
    slot_hot = iota((16, SLOTS), 0) == slot
    hot = jnp.concatenate([owner_hot.astype(F32), slot_hot.astype(F32)], axis=0).astype(BF16)
    earlier = dot(hot, before)
    owners = NYX * NZ
    rank = jnp.sum(jnp.where(owner_hot, earlier[0:owners], 0.0), axis=0, keepdims=True).astype(I32)
    if cap_rows < NYX * CAP:
        place = jnp.sum(jnp.where(slot_hot, earlier[owners:], 0.0), axis=0, keepdims=True).astype(I32)
    else:
        place = yx * CAP + rank
    over = jnp.max(jnp.where(place < cap_rows, 0.0, 1.0), axis=1, keepdims=True)
    row_of = slot * 8 + rank
    row_hot = (iota((NZ * 8, SLOTS), 0) == row_of).astype(F32).astype(BF16)
    yx_hot = iota((128, SLOTS), 0) == yx

    def spread(value):
        return dot_nt(row_hot, jnp.where(yx_hot, value.astype(F32), 0.0).astype(BF16))

    wanted = offset + 1
    message = (
        spread(jnp.bitwise_and(wanted, 63))
        + 64.0 * spread(lax.shift_right_logical(wanted, 6))
        + 8192.0 * spread(place)
    )
    message = message + jnp.where(jnp.bitwise_and(iota((NZ * 8, 128), 0), 7) == CAP, over, 0.0)
    ids_z[...] = message.reshape(NZ, 8, 128)
    candidate = slot * cap_rows + place

    pl.semaphore_wait(barrier, NZ - 1 + len(XY) + 1)

    for s, dz in enumerate(ORDER):
        if dz:
            pltpu.make_async_remote_copy(
                src_ref=ids_z.at[s], dst_ref=got_z.at[s], send_sem=z_send, recv_sem=z_recv,
                device_id=z_peer((my_z - dz + NZ) % NZ), device_id_type=MESH).start()
        else:
            got_z[s] = ids_z[s]

    def event_rows(first):
        rows = pl.ds(first, HALF // 2)
        pre = dot(hist_v[rows, :], we_v[...])
        states_v[rows, :] = (hist_v[rows, :].astype(F32) + jax.nn.gelu(pre)).astype(BF16)

    drain(got_z.at[pl.ds(0, NZ - 1)], z_recv)
    turn[...] = jnp.zeros_like(turn)
    for s in range(NZ):
        turn[s * CAP:(s + 1) * CAP, :] = got_z[s, 0:CAP, :]
    asked = turn[...]
    turned = jnp.transpose(asked)
    over = jnp.max(got_z[:, CAP, :], axis=0, keepdims=True)
    for n in range(NYX):
        ids_xy[n] = jnp.where(iota((8, 128), 0) == 0, turned[n:n + 1, :], over)
    for target in peers:
        pltpu.make_async_remote_copy(
            src_ref=ids_xy.at[target], dst_ref=got_xy.at[my_yx], send_sem=xy_send, recv_sem=xy_recv,
            device_id=xy_peer(target), device_id_type=MESH).start()
    got_xy[my_yx] = ids_xy[my_yx]

    for size, start, pos_row in zip(GROUPS, STARTS, pos_rows):
        for n in range(NYX):
            col[n * size:(n + 1) * size, :] = jnp.broadcast_to(asked[start:start + size, n:n + 1], (size, 128))
        pos_row[...] = jnp.transpose(col[0:NYX * size, :])

    load_hist.wait()
    load_we.wait()
    event_rows(0)
    event_rows(HALF // 2)

    drain(got_xy.at[pl.ds(0, NYX - 1)], xy_recv)
    turn[...] = jnp.zeros_like(turn)
    for n in range(NYX):
        turn[n:n + 1, :] = got_xy[n, 0:1, :]
    over = jnp.max(got_xy[:, 1, :], axis=0, keepdims=True)
    columns = jnp.bitwise_and(jnp.transpose(turn[...]).astype(I32), 8191)
    load_table.wait()

    lanes = iota((1, 128), 1) + 1
    chunk = 512
    for g, (size, start) in enumerate(zip(GROUPS, STARTS)):
        count = NYX * size
        wants = jnp.concatenate(
            [jnp.broadcast_to(columns[start:start + size, n:n + 1], (size, 128)) for n in range(NYX)], axis=0)
        total = None
        for first in range(0, ROWS, chunk):
            for block in range(0, chunk, 128):
                onehot[first // chunk, 0:count, block:block + 128] = jnp.where(
                    wants == lanes + (first + block), 1.0, 0.0).astype(BF16)
            term = dot(onehot[first // chunk, 0:count, :], table_v[first:first + chunk, :])
            total = term if total is None else total + term
        rows_xy[g][...] = total.astype(BF16).reshape(NYX, size, E)
        for target in peers:
            pltpu.make_async_remote_copy(
                src_ref=rows_xy[g].at[target], dst_ref=back_xy[g].at[my_yx],
                send_sem=rxy_send.at[g], recv_sem=rxy_recv.at[g],
                device_id=xy_peer(target), device_id_type=MESH).start()
        back_xy[g][my_yx] = rows_xy[g][my_yx]

    def z_copy(s, src, dst, plane):
        return pltpu.make_async_remote_copy(
            src_ref=src, dst_ref=dst, send_sem=rz_send, recv_sem=rz_recv.at[s],
            device_id=z_peer(plane), device_id_type=MESH)

    def forward(s):
        total = None
        for g, (size, start) in enumerate(zip(GROUPS, STARTS)):
            if (s + 1) * CAP <= start or s * CAP >= start + size:
                continue
            entries = pos_rows[g][0:cap_rows, :].astype(I32)
            here = lax.rem(iota((1, NYX * size), 1), size) + start
            mine = (here >= s * CAP) & (here < (s + 1) * CAP)
            filled = jnp.bitwise_and(entries, 8191) > 0
            pick = (lax.shift_right_logical(entries, 13) == iota((cap_rows, NYX * size), 0)) & filled & mine
            term = dot(pick.astype(F32).astype(BF16), back_xy[g][...].reshape(NYX * size, E))
            total = term if total is None else total + term
        if ORDER[s]:
            rows_z[s] = total.astype(BF16)
            z_copy(s, rows_z.at[s], back_z.at[s], (my_z + ORDER[s]) % NZ).start()
        else:
            back_z[s] = total.astype(BF16)

    def forward_group(g):
        drain(back_xy[g].at[pl.ds(0, NYX - 1)], rxy_recv.at[g])
        for s in range(NZ):
            if STARTS[g] < (s + 1) * CAP <= STARTS[g] + GROUPS[g]:
                forward(s)

    forward_group(0)

    load_wkv.wait()
    kv_v[section] = dot(states_v[...], wkv_v[...]).astype(BF16)
    kv_copy = pltpu.make_async_remote_copy(
        src_ref=kv_v.at[section], dst_ref=kv_v.at[section], send_sem=pair_send.at[0], recv_sem=pair_recv.at[0],
        device_id=other, device_id_type=MESH)
    kv_copy.start()

    load_query.wait()
    scale = 1.0 / math.sqrt(HEAD)
    length = len_ref[0]
    of_head = (iota((16, D), 1) // HEAD) == iota((16, D), 0)
    queries = jnp.where(of_head, query_v[...].astype(F32).reshape(1, D), 0.0).astype(BF16)
    events = section * HALF + iota((1, HALF), 1)
    pool_score = jnp.where(events < length, dot_nt(queries, states_v[...]) * scale, MASKED)
    pool_max = jnp.max(pool_score, axis=-1, keepdims=True)
    pool_exp = jnp.exp(pool_score - pool_max)
    pool_sum = jnp.sum(pool_exp, axis=-1, keepdims=True)
    pooled = dot(pool_exp.astype(BF16), states_v[...])

    def by_channel(x):
        return jnp.sum(jnp.where(of_head, x, 0.0), axis=0, keepdims=True)

    pool_mine[...] = jnp.concatenate(
        [by_channel(pooled), by_channel(pool_max), by_channel(pool_sum)]
        + [jnp.concatenate([over] * (D // 128), axis=1)] * 5, axis=0)
    pool_copy = pltpu.make_async_remote_copy(
        src_ref=pool_mine, dst_ref=pool_other, send_sem=pair_send.at[1], recv_sem=pair_recv.at[1],
        device_id=other, device_id_type=MESH)
    pool_copy.start()

    forward_group(1)

    pool_copy.wait_recv()
    mine, theirs = pool_mine[...], pool_other[...]
    first = jnp.where(section == 0, mine, theirs)
    second = jnp.where(section == 0, theirs, mine)
    joint = jnp.maximum(first[1:2], second[1:2])
    first_scale, second_scale = jnp.exp(first[1:2] - joint), jnp.exp(second[1:2] - joint)
    state = (first[0:1] * first_scale + second[0:1] * second_scale) / (
        first[2:3] * first_scale + second[2:3] * second_scale)
    state = state.astype(BF16)
    user_v[...] = state
    over_v[...] = jnp.maximum(mine[3:4, 0:128], theirs[3:4, 0:128])
    put_user = load(user_v, user_ref, 8)
    put_over = load(over_v, over_ref, 9)
    load_wr.wait()
    load_wout.wait()
    user_term = dot(jnp.broadcast_to(state, (16, D)), wr_v[2 * E:, :])[0:1]
    kv_copy.wait_recv()
    for k in range(2):
        keys_v[:, k * HALF:(k + 1) * HALF] = jnp.transpose(kv_v[k, :, 0:E])
        for h in range(E // HEAD):
            values_v[h, k * HALF:(k + 1) * HALF, 0:HEAD] = kv_v[k, :, E + h * HEAD:E + (h + 1) * HEAD]
            values_v[h, k * HALF:(k + 1) * HALF, HEAD:] = jnp.ones((HALF, HEAD), BF16)
    bias = jnp.where(iota((1, 2 * HALF), 1) < length, 0.0, MASKED)

    forward_group(2)
    drain(ids_z.at[pl.ds(0, NZ - 1)], z_send)
    drain(ids_xy.at[pl.ds(0, NYX - 1)], xy_send)
    for g in range(len(GROUPS)):
        drain(rows_xy[g].at[pl.ds(0, NYX - 1)], rxy_send.at[g])
    kv_copy.wait_send()
    pool_copy.wait_send()
    put_user.wait()
    put_over.wait()

    batch = 4 * cap_rows

    def attend(step, so_far):
        for s in (4 * step, 4 * step + 1, 4 * step + 2, 4 * step + 3):
            @pl.when(s != NZ - 1)
            def _():
                z_copy(s, rows_z.at[s], back_z.at[s], my_z).wait_recv()

        rows = back_z[pl.ds(4 * step, 4)].reshape(batch, E)

        def scores(h):
            return dot(rows[:, h * HEAD:(h + 1) * HEAD], keys_v[h * HEAD:(h + 1) * HEAD, :])

        heads_total = E // HEAD
        ready = scores(0)
        parts = []
        for h in range(heads_total):
            score = ready * (scale * math.log2(math.e)) + bias
            if h + 1 < heads_total:
                ready = scores(h + 1)
            expo = jnp.exp2(score - jnp.max(score, axis=-1, keepdims=True)).astype(BF16)
            early = dot(expo[:, 0:HALF], values_v[h, 0:HALF, :])
            late = dot(expo[:, HALF:], values_v[h, HALF:, :])
            inverse = 1.0 / (early[:, HEAD:] + late[:, HEAD:])
            early = (early[:, 0:HEAD] * inverse).astype(BF16).astype(F32)
            late = (late[:, 0:HEAD] * inverse).astype(BF16).astype(F32)
            parts.append((early + late).astype(BF16))
        attended = jnp.concatenate(parts, axis=-1)
        hidden = dot(rows, wr_v[0:E, :]) + dot(attended, wr_v[E:2 * E, :]) + user_term
        score = jnp.sum(jnp.maximum(hidden, 0.0) * wout_v[...].reshape(1, E), axis=-1, keepdims=True)
        mine = (iota((batch, SLOTS), 0) + step * batch) == candidate
        return so_far + jnp.sum(jnp.where(mine, score, 0.0), axis=0, keepdims=True)

    found = lax.fori_loop(0, NZ // 4, attend, jnp.zeros((1, SLOTS), F32))
    live = section * SLOTS + iota((1, SLOTS), 1) < count_ref[0]
    scores_ref[...] = jnp.where(live, found, 0.0)

    drain(rows_z.at[pl.ds(0, NZ - 1)], rz_send)


def fetch_and_rank(cap_rows, collective_id, hist_len, cand_ids, cand_count, pool_query, w_out, history, table,
                   w_event, w_kv, w_rank):
    vmem = pl.BlockSpec(memory_space=pltpu.VMEM)
    smem = pl.BlockSpec(memory_space=pltpu.SMEM)
    anywhere = pl.BlockSpec(memory_space=pl.ANY)
    dma = pltpu.SemaphoreType.DMA
    scratch = [
        pltpu.VMEM((1, SLOTS), I32), pltpu.VMEM((D,), BF16), pltpu.VMEM((E,), F32),
        pltpu.VMEM((1, D), BF16), pltpu.VMEM((1, 128), F32),
        pltpu.VMEM((HALF, D), BF16), pltpu.VMEM((ROWS, E), BF16), pltpu.VMEM((D, D), BF16),
        pltpu.VMEM((D, 2 * E), BF16), pltpu.VMEM((2 * E + D, E), BF16), pltpu.VMEM((HALF, D), BF16),
        pltpu.VMEM((2, HALF, 2 * E), BF16),
        pltpu.VMEM((NZ, 8, 128), F32), pltpu.VMEM((NZ, 8, 128), F32), pltpu.VMEM((128, 128), F32),
        pltpu.VMEM((NYX, 8, 128), F32), pltpu.VMEM((NYX, 8, 128), F32),
        pltpu.VMEM((NYX * max(GROUPS), 128), F32),
        [pltpu.VMEM((128, NYX * size), F32) for size in GROUPS],
        pltpu.VMEM((ROWS // 512, NYX * max(GROUPS), 512), BF16),
        [pltpu.VMEM((NYX, size, E), BF16) for size in GROUPS], [pltpu.VMEM((NYX, size, E), BF16) for size in GROUPS],
        pltpu.VMEM((NZ, cap_rows, E), BF16), pltpu.VMEM((NZ, cap_rows, E), BF16),
        pltpu.VMEM((8, D), F32), pltpu.VMEM((8, D), F32),
        pltpu.VMEM((E, 2 * HALF), BF16), pltpu.VMEM((E // HEAD, 2 * HALF, 2 * HEAD), BF16),
        dma((10,)), dma, dma, dma, dma, dma, dma((NZ,)),
        dma((len(GROUPS),)), dma((len(GROUPS),)), dma((2,)), dma((2,)),
    ]
    return pl.pallas_call(
        functools.partial(kernel, cap_rows),
        out_shape=(
            jax.ShapeDtypeStruct((1, SLOTS), F32), jax.ShapeDtypeStruct((1, D), BF16),
            jax.ShapeDtypeStruct((1, 128), F32)),
        in_specs=[smem, smem] + [anywhere] * 8,
        out_specs=(vmem, anywhere, anywhere),
        scratch_shapes=scratch,
        compiler_params=pltpu.CompilerParams(
            collective_id=collective_id, has_side_effects=True, vmem_limit_bytes=60 * 1024 * 1024),
        name="fetch_and_rank",
    )(hist_len, cand_count, cand_ids, pool_query, w_out, history, table, w_event, w_kv, w_rank)


def on_device(
    history, hist_len, cand_ids, cand_count, table, w_event, w_kv, pool_query, w_rank, w_out
):
    operands = (hist_len, cand_ids, cand_count, pool_query, w_out, history, table, w_event, w_kv, w_rank)
    scores, user_state, over = fetch_and_rank(ROOM, 0, *operands)
    scores = lax.cond(
        over[0, 0] > 0.0, lambda: fetch_and_rank(NYX * CAP, 1, *operands)[0], lambda: scores)
    return scores, user_state


def solution(mesh):
    placed = (
        P("item", "section", None),
        P("item"),
        P("item", "section"),
        P("item"),
        P("item", None),
        P(),
        P(),
        P(),
        P(),
        P(),
    )
    return jax.shard_map(
        on_device,
        mesh=mesh,
        in_specs=placed,
        out_specs=(P("item", "section"), P("item", None)),
        check_vma=False,
    )
```
